32 devices in a mesh: ctx: 8 (over z, y), head: 4 (over x, core).
Axes of the slice: x: 2, y: 2, z: 4, core: 2. Of those that a mesh axis runs over, the one named last changes fastest.
Arguments:
- queries: bfloat16 [4096, 32, 128], P(('ctx', 'head')), may hold values from -1.796875 to 1.796875
- key_vectors: bfloat16 [4096, 32, 128], P(('ctx', 'head')), may hold values from -1.796875 to 1.796875
- value_vectors: bfloat16 [4096, 32, 128], P(('ctx', 'head')), may hold values from -9.9 to 9.9
- output_grad: bfloat16 [4096, 32, 128], P(('ctx', 'head')), may hold values from -9.9 to 9.9
- decay_rate: float32 [32], replicated, may hold values from 0 to 1, as said below
- norm_gain: float32 [32, 128], replicated, may hold values from 0.25 to 1.75
Outputs:
- normed: bfloat16 [4096, 32, 128], P(('ctx', 'head'))
- query_gradient: bfloat16 [4096, 32, 128], P(('ctx', 'head'))
- grad_keys: bfloat16 [4096, 32, 128], P(('ctx', 'head'))
- value_gradient: bfloat16 [4096, 32, 128], P(('ctx', 'head'))
The draws below stay inside these ranges and needn't reach their ends.
Inputs may be any that keep to these rules, and one draw needn't show every extreme that they name: `decay_rate`: each head's rate is positive; a head's state is multiplied by exp(-rate) at every position.
All inputs are finite; a program needn't handle non-finite values.
Results may differ from the reference program's by a relative error of at most 0.012.
Values may be sent and summed in bfloat16 or wider, within the bound.
No kernel may reach another device: no remote copies, remote signals or barrier semaphores. Data moves between devices by JAX's collectives and lax.ppermute only.
A program may use at most 128 MiB of HBM per device.

```python
import math
import jax
import jax.numpy as jnp
from jax import lax

HD = 128
HEADS = 32
STRETCH = 128
TOKENS = 4096
N_CTX = 8
N_HEAD = 4


def draw_decay_rate(key, part):
    pick_key = jax.random.fold_in(key, 11)
    fast_key = jax.random.fold_in(key, 12)
    slow_key = jax.random.fold_in(key, 13)
    middle_key = jax.random.fold_in(key, 14)
    ordering = jax.random.permutation(pick_key, HEADS)
    fast_count = HEADS // 4
    middle_count = HEADS // 4
    is_fast = ordering < fast_count
    is_middle = jnp.logical_and(ordering >= fast_count, ordering < fast_count + middle_count)
    fast_rate = jnp.exp(jax.random.uniform(fast_key, (HEADS,), jnp.float32, math.log(1.0 / 50.0), math.log(1.0 / 30.0)))
    middle_rate = jnp.exp(jax.random.uniform(middle_key, (HEADS,), jnp.float32, math.log(1.0 / 2000.0), math.log(1.0 / 300.0)))
    slow_rate = jnp.exp(jax.random.uniform(slow_key, (HEADS,), jnp.float32, math.log(0.1), 0.0)) * (math.log(10.0) / TOKENS)
    return jnp.where(is_fast, fast_rate, jnp.where(is_middle, middle_rate, slow_rate)).astype(jnp.float32)


def stretch_levels(key):
    level_key = jax.random.fold_in(key, 21)
    exponent = jax.random.uniform(level_key, (TOKENS // STRETCH, 1, HEADS, 1), jnp.float32, -7.0, 0.5)
    return jnp.exp(exponent)


def leveled_draw(key, salt):
    entry_key = jax.random.fold_in(key, salt)
    shape = (TOKENS // STRETCH, STRETCH, HEADS, HD)
    base = jnp.clip(jax.random.normal(entry_key, shape, jnp.float32), -6.0, 6.0)
    return (base * stretch_levels(key)).reshape(TOKENS, HEADS, HD).astype(jnp.bfloat16)


def draw_value_vectors(key, part):
    return leveled_draw(key, 22)


def draw_output_grad(key, part):
    return leveled_draw(key, 23)


def shard_levels(key, shape, split, smallest, largest):
    def one(axis_at, shards_of):
        heights = jax.random.uniform(jax.random.fold_in(jax.random.fold_in(key, 6), axis_at), (shards_of,), jnp.float32, smallest / len(split), largest / len(split))
        return jnp.repeat(jnp.exp(heights), shape[axis_at] // shards_of).reshape((-1,) + (1,) * (len(shape) - axis_at - 1))

    gain = one(*split[0])
    for cut in split[1:]:
        gain = gain * one(*cut)
    return gain


def centred(own_key, dims, scale, reach, pieces=(), dtype=jnp.bfloat16):
    drawn = scale * jax.random.normal(own_key, dims, jnp.float32)
    if pieces:
        drawn = drawn * shard_levels(own_key, dims, pieces, -0.22, 0.18)
    return jnp.clip(drawn, -reach, reach).astype(dtype)


def setup_inputs(seed: int = 0) -> dict:
    keys = jax.random.split(jax.random.key(seed), 7)
    queries = centred(keys[0], (TOKENS, HEADS, HD), 0.3, 1.796875, ((0, 32),))
    key_vectors = centred(keys[1], (TOKENS, HEADS, HD), 0.3, 1.796875, ((0, 32),))
    value_vectors = draw_value_vectors(jax.random.fold_in(keys[6], 71), 0)
    output_grad = draw_output_grad(jax.random.fold_in(keys[6], 71), 0)
    decay_rate = draw_decay_rate(jax.random.fold_in(keys[6], 71), 0)
    norm_gain = jnp.clip(1.0 + 0.15 * jax.random.normal(keys[5], (HEADS, HD), jnp.float32), 0.25, 1.75)
    return {"queries": queries, "key_vectors": key_vectors, "value_vectors": value_vectors, "output_grad": output_grad, "decay_rate": decay_rate, "norm_gain": norm_gain}


def carry_stretches(stretch_states, decay_value, length, forward):
    stretch_order = jnp.arange(N_HEAD).astype(jnp.float32)
    place_in = stretch_order if forward else N_HEAD - 1.0 - stretch_order
    states_float = stretch_states.astype(jnp.float32)
    fold_weights = jnp.exp(-decay_value * length * (N_HEAD - 1.0 - place_in))
    block_state = jnp.einsum('k,bkde->bde', fold_weights, states_float, precision=lax.Precision.HIGHEST).astype(jnp.bfloat16).astype(jnp.float32)
    span_decay = jnp.exp(-decay_value * length * N_HEAD)

    def carry_step(state, piece):
        return (span_decay * state + piece, state)
    empty_state = jnp.zeros(block_state.shape[1:], jnp.float32)
    final_state, carried = lax.scan(carry_step, empty_state, block_state, reverse=not forward)
    lead_decay = jnp.exp(-decay_value * length * place_in)
    stretch_gap = place_in[:, None] - 1.0 - place_in[None, :]
    inner_weights = jnp.where(stretch_gap >= 0, jnp.exp(-decay_value * length * jnp.maximum(stretch_gap, 0.0)), 0.0)
    spread = lead_decay[None, :, None, None] * carried[:, None] + jnp.einsum('kq,bqde->bkde', inner_weights, states_float, precision=lax.Precision.HIGHEST)
    return spread.reshape(N_CTX * N_HEAD, HD, HD).astype(jnp.bfloat16).astype(jnp.float32)

def one_head(operands):
    query_blocks, key_blocks, value_blocks, grad_blocks, decay_value, gain_row = operands
    length = query_blocks.shape[1]
    head_size = query_blocks.shape[2]
    steps = jnp.arange(length).astype(jnp.float32)
    offset = steps[:, None] - steps[None, :]
    decay_weight_mask = jnp.where(offset >= 0, jnp.exp(-decay_value * jnp.maximum(offset, 0.0)), 0.0)
    per_head_decay = jnp.exp(-decay_value * (steps + 1.0))[:, None]
    trailing_decay = jnp.exp(-decay_value * (length - 1.0 - steps))[:, None]
    query_widened = query_blocks.astype(jnp.float32)
    key_widened = key_blocks.astype(jnp.float32)
    value_widened = value_blocks.astype(jnp.float32)
    scores = jnp.einsum('nid,njd->nij', query_widened, key_widened)
    attention_matrix = (scores * decay_weight_mask).astype(jnp.bfloat16)
    key_decayed = (key_widened * trailing_decay).astype(jnp.bfloat16)
    local_state = jnp.einsum('njd,nje->nde', key_decayed.astype(jnp.float32), value_widened).astype(jnp.bfloat16)
    incoming_portion = carry_stretches(local_state.reshape(N_CTX, N_HEAD, head_size, head_size), decay_value, length * 1.0, True)
    output_rows = jnp.einsum('ywt,ytg->ywg', attention_matrix.astype(jnp.float32), value_widened)
    output_rows = output_rows + per_head_decay * jnp.einsum('wbr,wrx->wbx', query_widened, incoming_portion)
    inv_rms = lax.rsqrt(lax.optimization_barrier(jnp.mean(output_rows * output_rows, axis=-1, keepdims=True)) + 1e-06)
    unit_rows = output_rows * inv_rms
    normed = (unit_rows * gain_row).astype(jnp.bfloat16)
    scaled = gain_row * grad_blocks.astype(jnp.float32)
    grad_out = (inv_rms * (scaled - unit_rows * lax.optimization_barrier(jnp.mean(scaled * unit_rows, axis=-1, keepdims=True)))).astype(jnp.bfloat16)
    gradient_widened = grad_out.astype(jnp.float32)
    query_with_decay = (query_widened * per_head_decay).astype(jnp.bfloat16)
    state_gradient = jnp.einsum('lou,loz->luz', query_with_decay.astype(jnp.float32), gradient_widened).astype(jnp.bfloat16)
    later_portion = carry_stretches(state_gradient.reshape(N_CTX, N_HEAD, head_size, head_size), decay_value, length * 1.0, False)
    score_gradient = (jnp.einsum('vuy,vsy->vus', gradient_widened, value_widened) * decay_weight_mask).astype(jnp.bfloat16).astype(jnp.float32)
    query_gradient = jnp.einsum('zwc,zca->zwa', score_gradient, key_widened) + per_head_decay * jnp.einsum('rcq,rwq->rcw', gradient_widened, incoming_portion)
    grad_keys = jnp.einsum('nij,nid->njd', score_gradient, query_widened) + trailing_decay * jnp.einsum('nje,nde->njd', value_widened, later_portion)
    value_gradient = jnp.einsum('qml,qmb->qlb', attention_matrix.astype(jnp.float32), gradient_widened) + trailing_decay * jnp.einsum('opv,ovr->opr', key_widened, later_portion)
    return (normed, query_gradient.astype(jnp.bfloat16), grad_keys.astype(jnp.bfloat16), value_gradient.astype(jnp.bfloat16))

def reference(queries, key_vectors, value_vectors, output_grad, decay_rate, norm_gain):

    def to_heads(array):
        return array.reshape(N_CTX * N_HEAD, STRETCH, HEADS, HD).transpose(2, 0, 1, 3)

    def to_tokens(array):
        return array.transpose(1, 2, 0, 3).reshape(TOKENS, HEADS, HD)
    results = lax.map(one_head, (to_heads(queries), to_heads(key_vectors), to_heads(value_vectors), to_heads(output_grad), decay_rate.astype(jnp.float32), norm_gain.astype(jnp.float32)))
    return (to_tokens(results[0]), to_tokens(results[1]), to_tokens(results[2]), to_tokens(results[3]))
```

```python
import functools
import jax
import jax.numpy as jnp
from jax import lax
from jax.experimental import pallas as pl
from jax.experimental.pallas import tpu as pltpu
from jax.sharding import PartitionSpec as P

AXES = ("ctx", "head")
F32 = jnp.float32
BF16 = jnp.bfloat16
VMEM_LIMIT = 48 * 1024 * 1024


def dot(a, b, dims):
    return lax.dot_general(a, b, (dims, ((), ())), preferred_element_type=F32)


AB = ((1,), (0,))
ABT = ((1,), (1,))
ATB = ((0,), (0,))


def decay(rate, steps):
    return jnp.exp(-rate * steps)


def positions(shape):
    return lax.broadcasted_iota(jnp.int32, shape, 0).astype(F32)


def causal_weights(rate, length):
    row = lax.broadcasted_iota(jnp.int32, (length, length), 0)
    col = lax.broadcasted_iota(jnp.int32, (length, length), 1)
    offset = (row - col).astype(F32)
    return jnp.where(offset >= 0, jnp.exp(-rate * jnp.maximum(offset, 0.0)), 0.0)


def split_heads(block_ref, scratch):
    length, heads, size = block_ref.shape
    scratch[...] = block_ref[...].astype(F32).reshape(length * heads, size)


def one_head(scratch, h, length, heads):
    return scratch[pl.ds(h, length, stride=heads), :]


def join_heads(scratch, out_ref):
    out_ref[...] = scratch[...].reshape(out_ref.shape).astype(out_ref.dtype)


def local_kernel(meta, k_ref, v_ref, rate_ref, kt_ref, vt_ref, s_ref, ks, vs):
    length, heads, size = k_ref.shape
    split_heads(k_ref, ks)
    split_heads(v_ref, vs)
    first = meta[0] * heads
    tail_steps = length - 1.0 - positions((length, size))
    for h in range(heads):
        key = one_head(ks, h, length, heads)
        value = one_head(vs, h, length, heads).astype(BF16)
        kt_ref[h] = key.astype(BF16)
        vt_ref[h] = value
        rate = rate_ref[pl.ds(first + h, 1), :]
        key_decayed = (key * decay(rate, tail_steps)).astype(BF16)
        s_ref[h] = dot(key_decayed, value, ATB).astype(BF16)


def attention_kernel(meta, q_ref, g_ref, kt_ref, vt_ref, rate_ref, qt_ref, gt_ref, a_ref, o_ref, qs, gs):
    length, heads, size = q_ref.shape
    split_heads(q_ref, qs)
    split_heads(g_ref, gs)
    first = meta[0] * heads
    for h in range(heads):
        query = one_head(qs, h, length, heads).astype(BF16)
        qt_ref[h] = query
        gt_ref[h] = one_head(gs, h, length, heads).astype(BF16)
        rate = rate_ref[pl.ds(first + h, 1), :]
        scores = dot(query, kt_ref[h], ABT)
        attention = (scores * causal_weights(rate, length)).astype(BF16)
        a_ref[h] = attention
        o_ref[h] = dot(attention, vt_ref[h], AB)


def norm_kernel(meta, qt_ref, gt_ref, o_ref, in_ref, rate_ref, gain_ref, n_ref, go_ref, sg_ref):
    heads, length, size = qt_ref.shape
    first = meta[0] * heads
    head_steps = positions((length, size)) + 1.0
    for h in range(heads):
        rate = rate_ref[pl.ds(first + h, 1), :]
        gain = gain_ref[pl.ds(first + h, 1), :]
        head_decay = decay(rate, head_steps)
        query = qt_ref[h]
        out = o_ref[h] + head_decay * dot(query, in_ref[h], AB)
        inv_rms = lax.rsqrt(jnp.mean(out * out, axis=-1, keepdims=True) + 1e-06)
        unit = out * inv_rms
        n_ref[h] = (unit * gain).astype(BF16)
        scaled = gain * gt_ref[h].astype(F32)
        grad_out = (inv_rms * (scaled - unit * jnp.mean(scaled * unit, axis=-1, keepdims=True))).astype(BF16)
        go_ref[h] = grad_out
        query_decayed = (query.astype(F32) * head_decay).astype(BF16)
        sg_ref[h] = dot(query_decayed, grad_out, ATB).astype(BF16)


def grad_kernel(meta, qt_ref, kt_ref, vt_ref, a_ref, go_ref, in_ref, n_ref, rate_ref, *rest):
    n_out, dq_out, dk_ref, dv_ref, ns, ds = rest[-6:]
    heads, length, size = qt_ref.shape
    first = meta[0] * heads
    head_steps = positions((length, size)) + 1.0
    for h in range(heads):
        rate = rate_ref[pl.ds(first + h, 1), :]
        grad_out = go_ref[h]
        grad_scores = (dot(grad_out, vt_ref[h], ABT) * causal_weights(rate, length)).astype(BF16)
        through_state = dot(grad_out, in_ref[h], ABT)
        ds[pl.ds(h, length, stride=heads), :] = (
            dot(grad_scores, kt_ref[h], AB) + decay(rate, head_steps) * through_state
        )
        ns[pl.ds(h, length, stride=heads), :] = n_ref[h].astype(F32)
        dk_ref[h] = dot(grad_scores, qt_ref[h], ATB)
        dv_ref[h] = dot(a_ref[h], grad_out, ATB)
    join_heads(ns, n_out)
    join_heads(ds, dq_out)


def later_kernel(meta, kt_ref, vt_ref, later_ref, dk_ref, dv_ref, rate_ref, *rest):
    dk_out, dv_out, ks, vs = rest[-4:]
    heads, length, size = kt_ref.shape
    first = meta[0] * heads
    tail_steps = length - 1.0 - positions((length, size))
    for h in range(heads):
        tail = decay(rate_ref[pl.ds(first + h, 1), :], tail_steps)
        later = later_ref[h]
        ks[pl.ds(h, length, stride=heads), :] = dk_ref[h] + tail * dot(vt_ref[h], later, ABT)
        vs[pl.ds(h, length, stride=heads), :] = dv_ref[h] + tail * dot(kt_ref[h], later, AB)
    join_heads(ks, dk_out)
    join_heads(vs, dv_out)


def row_weight(rate, span, steps):
    weight = jnp.exp(-rate * (span * jnp.maximum(steps, 0).astype(F32)))
    return jnp.where(steps >= 0, weight, 0.0)


def fold_kernel(group, next_group, span, meta, rate_ref, *refs):
    states, parts = refs[:group], refs[group:]
    heads = parts[0].shape[0]
    for k in range(next_group):
        start = (meta[2] ^ k) * heads
        for i in range(heads):
            rate = rate_ref[pl.ds(meta[0] + start + i, 1), :]
            total = None
            for j in range(group):
                weight = row_weight(rate, span, group - 1 - (meta[1] ^ j))
                term = weight * states[j][start + i].astype(F32)
                total = term if total is None else total + term
            parts[k][i] = total.astype(BF16)


def spread_kernel(group, next_group, top, span, meta, rate_ref, *refs):
    states, ahead, outs = refs[:group], refs[group:-group], refs[-group:]
    heads = states[0].shape[0]
    part_heads = heads if top else heads // next_group
    for k in range(1 if top else next_group):
        start = 0 if top else (meta[2] ^ k) * part_heads
        for i in range(part_heads):
            rate = rate_ref[pl.ds(meta[0] + start + i, 1), :]
            if top:
                before = None
                for j in range(1, next_group):
                    weight = row_weight(rate, span * group, meta[2] - 1 - (meta[2] ^ j))
                    term = weight * ahead[j - 1][i].astype(F32)
                    before = term if before is None else before + term
            else:
                before = ahead[k][i].astype(F32)
            own = [states[j][start + i].astype(F32) for j in range(group)]
            for j in range(group):
                place = meta[1] ^ j
                total = row_weight(rate, span, place) * before
                for q in range(group):
                    if q != j:
                        total = total + row_weight(rate, span, place - 1 - (meta[1] ^ q)) * own[q]
                outs[j][start + i] = total.astype(BF16)


def call(body, meta, inputs, outputs, scratch=(), aliases=None, flops=0, name=None):
    def spec(shape, block):
        if block == "any":
            return pl.BlockSpec(memory_space=pl.ANY)
        if block is None:
            return pl.BlockSpec(shape, lambda i, m: (0,) * len(shape))
        return pl.BlockSpec(block, lambda i, m: (0, m[0], 0))

    nbytes = sum(a.size * a.dtype.itemsize for a, _ in inputs)
    nbytes += sum(s.size * s.dtype.itemsize for s, _ in outputs)
    return pl.pallas_call(
        body,
        grid_spec=pltpu.PrefetchScalarGridSpec(
            num_scalar_prefetch=1,
            grid=(1,),
            in_specs=[spec(a.shape, b) for a, b in inputs],
            out_specs=[spec(s.shape, b) for s, b in outputs],
            scratch_shapes=list(scratch),
        ),
        out_shape=[s for s, _ in outputs],
        input_output_aliases=aliases or {},
        compiler_params=pltpu.CompilerParams(vmem_limit_bytes=VMEM_LIMIT),
        cost_estimate=pl.CostEstimate(flops=flops, bytes_accessed=nbytes, transcendentals=0),
        name=name,
    )(meta, *[a for a, _ in inputs])


def level_sizes(devices):
    sizes = [2]
    left = devices // 2
    while left > 8:
        sizes.append(4)
        left //= 4
    return sizes + [left]


def swap(array, distance, devices):
    return lax.ppermute(array, AXES, [(i, i ^ distance) for i in range(devices)])


def carry_states(kept, sent, index, devices, rates, first_head, length, forward):
    sizes = level_sizes(devices)
    state = kept.shape[1:]
    places, lows = [], []
    low = 1
    for size in sizes:
        places.append((index // low) % size)
        lows.append(low)
        low *= size

    def weigh_place(level):
        return places[level] if forward else places[level] ^ (sizes[level] - 1)

    def climb(level, parts, first):
        group, next_group = sizes[level], sizes[level + 1]
        top = level + 2 == len(sizes)
        span = float(length * lows[level])
        states = [parts[0]] + [swap(parts[k], k * lows[level], devices) for k in range(1, group)]
        heads = parts[0].shape[0]
        part_heads = heads if top else heads // next_group
        next_place = 0 if top else places[level + 1]
        meta = jnp.stack([first, weigh_place(level), next_place + 0 * first]).astype(jnp.int32)
        count = 1 if top else next_group
        folded = call(
            functools.partial(fold_kernel, group, count, span),
            meta,
            [(rates, None)] + [(s, None) for s in states],
            [(jax.ShapeDtypeStruct((part_heads,) + state, BF16), None)] * count,
            name="fold_states",
        )
        if top:
            distance = lows[level + 1]
            ahead = [swap(folded[0], k * distance, devices) for k in range(1, next_group)]
            next_meta = weigh_place(level + 1)
        else:
            ahead = climb(level + 1, folded, first + next_place * part_heads)
            next_meta = next_place
        meta = jnp.stack([first, weigh_place(level), next_meta]).astype(jnp.int32)
        outs = call(
            functools.partial(spread_kernel, group, next_group, top, span),
            meta,
            [(rates, None)] + [(s, None) for s in states] + [(a, None) for a in ahead],
            [(jax.ShapeDtypeStruct((heads,) + state, BF16), None)] * group,
            name="spread_states",
        )
        return [outs[0]] + [swap(outs[k], k * lows[level], devices) for k in range(1, group)]

    return climb(0, [kept, sent], first_head)


def local(devices, queries, key_vectors, value_vectors, output_grad, decay_rate, norm_gain):
    length, heads, size = queries.shape
    half = heads // 2
    index = lax.axis_index("ctx") * lax.axis_size("head") + lax.axis_index("head")
    core = index % 2
    rates = jnp.broadcast_to(decay_rate[:, None], (heads, size))
    block = (length, half, size)
    per_head = (half, length, size)
    states = (half, size, size)

    def shaped(shape, dtype=BF16):
        return (jax.ShapeDtypeStruct(shape, dtype), None)

    def flat():
        return pltpu.VMEM((length * half, size), F32)

    def whole():
        return (jax.ShapeDtypeStruct(queries.shape, BF16), block)

    unit = 2 * half * length * size * size
    metas = [jnp.reshape(core, (1,)).astype(jnp.int32), jnp.reshape(1 - core, (1,)).astype(jnp.int32)]

    keys, values, local_states = [None, None], [None, None], [None, None]
    for s in (1, 0):
        keys[s], values[s], local_states[s] = call(
            local_kernel,
            metas[s],
            [(key_vectors, block), (value_vectors, block), (rates, None)],
            [shaped(per_head), shaped(per_head), shaped(states)],
            [flat(), flat()],
            flops=unit,
            name="local_states",
        )
    incoming = carry_states(
        local_states[0], local_states[1], index, devices, rates, core * half, length, True
    )
    query, grad, attention, inner = [None, None], [None, None], [None, None], [None, None]
    for s in (0, 1):
        query[s], grad[s], attention[s], inner[s] = call(
            attention_kernel,
            metas[s],
            [(queries, block), (output_grad, block), (keys[s], None), (values[s], None), (rates, None)],
            [shaped(per_head), shaped(per_head), shaped((half, length, length)), shaped(per_head, F32)],
            [flat(), flat()],
            flops=2 * unit,
            name="attention",
        )
    normed, grad_out, state_grad = [None, None], [None, None], [None, None]
    for s in (0, 1):
        normed[s], grad_out[s], state_grad[s] = call(
            norm_kernel,
            metas[s],
            [
                (query[s], None),
                (grad[s], None),
                (inner[s], None),
                (incoming[s], None),
                (rates, None),
                (norm_gain, None),
            ],
            [shaped(per_head), shaped(per_head), shaped(states)],
            flops=2 * unit,
            name="norm",
        )
    later = carry_states(
        state_grad[1], state_grad[0], index, devices, rates, (1 - core) * half, length, False
    )
    normed_out, query_out, key_part, value_part = None, None, [None, None], [None, None]
    for s in (0, 1):
        inputs = [
            (query[s], None),
            (keys[s], None),
            (values[s], None),
            (attention[s], None),
            (grad_out[s], None),
            (incoming[s], None),
            (normed[s], None),
            (rates, None),
        ]
        aliases = {}
        if s:
            aliases = {1 + len(inputs): 0, 2 + len(inputs): 1}
            inputs += [(normed_out, "any"), (query_out, "any")]
        normed_out, query_out, key_part[s], value_part[s] = call(
            grad_kernel,
            metas[s],
            inputs,
            [whole(), whole(), shaped(per_head, F32), shaped(per_head, F32)],
            [flat(), flat()],
            aliases,
            flops=5 * unit,
            name="stretch_gradients",
        )
    key_out, value_out = None, None
    for s in (1, 0):
        inputs = [
            (keys[s], None),
            (values[s], None),
            (later[1 - s], None),
            (key_part[s], None),
            (value_part[s], None),
            (rates, None),
        ]
        aliases = {}
        if s == 0:
            aliases = {1 + len(inputs): 0, 2 + len(inputs): 1}
            inputs += [(key_out, "any"), (value_out, "any")]
        key_out, value_out = call(
            later_kernel,
            metas[s],
            inputs,
            [whole(), whole()],
            [flat(), flat()],
            aliases,
            flops=2 * unit,
            name="later_gradients",
        )
    return normed_out, query_out, key_out, value_out


def solution(mesh):
    devices = mesh.shape["ctx"] * mesh.shape["head"]
    spread = P(AXES, None, None)
    return jax.shard_map(
        functools.partial(local, devices),
        mesh=mesh,
        in_specs=(spread, spread, spread, spread, P(), P()),
        out_specs=(spread, spread, spread, spread),
        check_vma=False,
    )
```

```python
import functools
import jax
import jax.numpy as jnp
from jax import lax
from jax.experimental import pallas as pl
from jax.experimental.pallas import tpu as pltpu
from jax.sharding import PartitionSpec as P

AXES = ("ctx", "head")
F32 = jnp.float32
BF16 = jnp.bfloat16
VMEM_LIMIT = 16 * 1024 * 1024
BATCH = 4
CHUNKS = 4


def dot(a, b, dims):
    return lax.dot_general(a, b, (dims, ((), ())), preferred_element_type=F32)


AB = ((1,), (0,))
ABT = ((1,), (1,))
ATB = ((0,), (0,))


def decay(rate, steps):
    return jnp.exp(-rate * steps)


def positions(shape):
    return lax.broadcasted_iota(jnp.int32, shape, 0).astype(F32)


def causal_weights(rate, length):
    row = lax.broadcasted_iota(jnp.int32, (length, length), 0)
    col = lax.broadcasted_iota(jnp.int32, (length, length), 1)
    offset = (row - col).astype(F32)
    return jnp.where(offset >= 0, jnp.exp(-rate * jnp.maximum(offset, 0.0)), 0.0)


def my_index():
    return lax.axis_index("ctx") * lax.axis_size("head") + lax.axis_index("head")


def head_half(own):
    core = my_index() % 2
    return core if own else 1 - core


def split_heads(block_ref, scratch, half, heads):
    length, _, size = block_ref.shape
    start = pl.multiple_of(half * heads, heads)
    scratch[...] = block_ref[:, pl.ds(start, heads), :].astype(F32).reshape(length * heads, size)


def one_head(scratch, h, length, heads):
    return scratch[pl.ds(h, length, stride=heads), :]


def start_output(scratch, stage, out_ref, sems, half):
    length, heads, size = stage.shape
    chunks = sems.shape[0]
    rows = length // chunks
    start = pl.multiple_of(half * heads, heads)
    copies = []
    for c in range(chunks):
        piece = pl.ds(c * rows, rows)
        stage[piece] = scratch[pl.ds(c * rows * heads, rows * heads), :].reshape(rows, heads, size).astype(BF16)
        copy = pltpu.make_async_copy(stage.at[piece], out_ref.at[piece, pl.ds(start, heads), :], sems.at[c])
        copy.start()
        copies.append(copy)
    return copies


def batches(heads, size=BATCH):
    size = min(size, heads)
    return [range(start, start + size) for start in range(0, heads, size)]


def local_kernel(own, k_ref, v_ref, rate_ref, kt_ref, vt_ref, s_ref, kb, vb, ks, vs, sems):
    length, heads, size = kb.shape
    half = head_half(own)
    first = half * heads
    start = pl.multiple_of(first, heads)
    chunks = sems.shape[1]
    rows = length // chunks
    copies = []
    for c in range(chunks):
        piece = pl.ds(c * rows, rows)
        for n, (ref, buffer) in enumerate(((k_ref, kb), (v_ref, vb))):
            copy = pltpu.make_async_copy(ref.at[piece, pl.ds(start, heads), :], buffer.at[piece], sems.at[n, c])
            copy.start()
            copies.append(copy)
    for c in range(chunks):
        piece = pl.ds(c * rows, rows)
        flat = pl.ds(c * rows * heads, rows * heads)
        copies[2 * c].wait()
        ks[flat, :] = kb[piece].astype(F32).reshape(rows * heads, size)
        copies[2 * c + 1].wait()
        vs[flat, :] = vb[piece].astype(F32).reshape(rows * heads, size)
    tail_steps = length - 1.0 - positions((length, size))
    for batch in batches(heads):
        key = [one_head(ks, h, length, heads) for h in batch]
        value = [one_head(vs, h, length, heads).astype(BF16) for h in batch]
        tail = [decay(rate_ref[pl.ds(first + h, 1), :], tail_steps) for h in batch]
        decayed = [(k * t).astype(BF16) for k, t in zip(key, tail)]
        state = [dot(k, v, ATB) for k, v in zip(decayed, value)]
        for i, h in enumerate(batch):
            kt_ref[h] = key[i].astype(BF16)
            vt_ref[h] = value[i]
            s_ref[h] = state[i].astype(BF16)


def attention_kernel(own, q_ref, g_ref, kt_ref, vt_ref, rate_ref, qt_ref, gt_ref, a_ref, o_ref, qs, gs):
    heads, length, size = kt_ref.shape
    half = head_half(own)
    first = half * heads
    split_heads(q_ref, qs, half, heads)
    split_heads(g_ref, gs, half, heads)
    for batch in batches(heads):
        query = [one_head(qs, h, length, heads).astype(BF16) for h in batch]
        scores = [dot(q, kt_ref[h], ABT) for q, h in zip(query, batch)]
        weights = [causal_weights(rate_ref[pl.ds(first + h, 1), :], length) for h in batch]
        attention = [(s * w).astype(BF16) for s, w in zip(scores, weights)]
        inner = [dot(a, vt_ref[h], AB) for a, h in zip(attention, batch)]
        for i, h in enumerate(batch):
            qt_ref[h] = query[i]
            gt_ref[h] = one_head(gs, h, length, heads).astype(BF16)
            a_ref[h] = attention[i]
            o_ref[h] = inner[i]


def norm_kernel(own, qt_ref, gt_ref, o_ref, in_ref, rate_ref, gain_ref, n_ref, go_ref, sg_ref):
    heads, length, size = qt_ref.shape
    first = head_half(own) * heads
    head_steps = positions((length, size)) + 1.0
    for batch in batches(heads):
        through = [dot(qt_ref[h], in_ref[h], AB) for h in batch]
        head_decay = [decay(rate_ref[pl.ds(first + h, 1), :], head_steps) for h in batch]
        out = [o_ref[h] + d * t for h, d, t in zip(batch, head_decay, through)]
        inv_rms = [lax.rsqrt(jnp.mean(o * o, axis=-1, keepdims=True) + 1e-06) for o in out]
        unit = [o * r for o, r in zip(out, inv_rms)]
        gain = [gain_ref[pl.ds(first + h, 1), :] for h in batch]
        scaled = [g * gt_ref[h].astype(F32) for g, h in zip(gain, batch)]
        along = [jnp.mean(s * u, axis=-1, keepdims=True) for s, u in zip(scaled, unit)]
        grad_out = [
            (r * (s - u * m)).astype(BF16) for r, s, u, m in zip(inv_rms, scaled, unit, along)
        ]
        decayed = [(qt_ref[h].astype(F32) * d).astype(BF16) for h, d in zip(batch, head_decay)]
        state = [dot(q, g, ATB) for q, g in zip(decayed, grad_out)]
        for i, h in enumerate(batch):
            n_ref[h] = (unit[i] * gain[i]).astype(BF16)
            go_ref[h] = grad_out[i]
            sg_ref[h] = state[i].astype(BF16)


def grad_kernel(own, qt_ref, kt_ref, vt_ref, a_ref, go_ref, in_ref, n_ref, rate_ref, *rest):
    n_out, dq_out, dk_ref, dv_ref, ns, ds, nb, db, sems = rest[-9:]
    heads, length, size = qt_ref.shape
    half = head_half(own)
    first = half * heads
    head_steps = positions((length, size)) + 1.0
    for h in range(heads):
        ns[pl.ds(h, length, stride=heads), :] = n_ref[h].astype(F32)
    copies = start_output(ns, nb, n_out, sems.at[0], half)
    for batch in batches(heads):
        inner = [dot(go_ref[h], vt_ref[h], ABT) for h in batch]
        through = [dot(go_ref[h], in_ref[h], ABT) for h in batch]
        value = [dot(a_ref[h], go_ref[h], ATB) for h in batch]
        rate = [rate_ref[pl.ds(first + h, 1), :] for h in batch]
        scores = [(s * causal_weights(r, length)).astype(BF16) for s, r in zip(inner, rate)]
        query = [dot(s, kt_ref[h], AB) for s, h in zip(scores, batch)]
        key = [dot(s, qt_ref[h], ATB) for s, h in zip(scores, batch)]
        for i, h in enumerate(batch):
            dv_ref[h] = value[i]
            dk_ref[h] = key[i]
            ds[pl.ds(h, length, stride=heads), :] = query[i] + decay(rate[i], head_steps) * through[i]
    copies += start_output(ds, db, dq_out, sems.at[1], half)
    for copy in copies:
        copy.wait()


def later_kernel(own, kt_ref, vt_ref, later_ref, dk_ref, dv_ref, rate_ref, *rest):
    dk_out, dv_out, ks, vs, kb, vb, sems = rest[-7:]
    heads, length, size = kt_ref.shape
    half = head_half(own)
    first = half * heads
    tail_steps = length - 1.0 - positions((length, size))
    for batch in batches(heads):
        key = [dot(vt_ref[h], later_ref[h], ABT) for h in batch]
        value = [dot(kt_ref[h], later_ref[h], AB) for h in batch]
        for i, h in enumerate(batch):
            tail = decay(rate_ref[pl.ds(first + h, 1), :], tail_steps)
            ks[pl.ds(h, length, stride=heads), :] = dk_ref[h] + tail * key[i]
            vs[pl.ds(h, length, stride=heads), :] = dv_ref[h] + tail * value[i]
    copies = start_output(ks, kb, dk_out, sems.at[0], half)
    copies += start_output(vs, vb, dv_out, sems.at[1], half)
    for copy in copies:
        copy.wait()


def row_weight(rate, span, steps):
    weight = jnp.exp(-rate * (span * jnp.maximum(steps, 0).astype(F32)))
    return jnp.where(steps >= 0, weight, 0.0)


def place_at(sizes, level, forward=True):
    low = 1
    for size in sizes[:level]:
        low *= size
    place = (my_index() // low) % sizes[level]
    return place if forward else place ^ (sizes[level] - 1)


def first_head(sizes, level, heads, forward):
    first, count = 0, heads
    for above in range(level + 1):
        count //= sizes[above]
        place = place_at(sizes, above)
        if above == 0 and not forward:
            place = 1 - place
        first = first + place * count
    return first


def fold_kernel(sizes, level, span, forward, rate_ref, *refs):
    group = sizes[level]
    top = level + 2 == len(sizes)
    states = refs[:group]
    parts = refs[group : group + 1] if top else refs[-sizes[level + 1] :]
    if top:
        parts = refs[-1:]
    heads = parts[0].shape[0]
    first = first_head(sizes, level, rate_ref.shape[0], forward)
    place = place_at(sizes, level, forward)
    weigh = [group - 1 - (place ^ j) for j in range(group)]
    for k in range(len(parts)):
        start = 0 if top else (place_at(sizes, level + 1) ^ k) * heads
        for i in range(heads):
            rate = rate_ref[pl.ds(first + start + i, 1), :]
            total = None
            for j in range(group):
                term = row_weight(rate, span, weigh[j]) * states[j][start + i].astype(F32)
                total = term if total is None else total + term
            parts[k][i] = total.astype(BF16)


def spread_kernel(sizes, level, span, forward, rate_ref, *refs):
    group, next_group = sizes[level], sizes[level + 1]
    top = level + 2 == len(sizes)
    ahead_count = next_group - 1 if top else next_group
    states, ahead, outs = refs[:group], refs[group : group + ahead_count], refs[-group:]
    heads = states[0].shape[0]
    part_heads = heads if top else heads // next_group
    first = first_head(sizes, level, rate_ref.shape[0], forward)
    place = place_at(sizes, level, forward)
    top_place = place_at(sizes, level + 1, forward)
    for k in range(1 if top else next_group):
        start = 0 if top else (place_at(sizes, level + 1) ^ k) * part_heads
        for i in range(part_heads):
            rate = rate_ref[pl.ds(first + start + i, 1), :]
            if top:
                before = None
                for j in range(1, next_group):
                    weight = row_weight(rate, span * group, top_place - 1 - (top_place ^ j))
                    term = weight * ahead[j - 1][i].astype(F32)
                    before = term if before is None else before + term
            else:
                before = ahead[k][i].astype(F32)
            own = [states[j][start + i].astype(F32) for j in range(group)]
            for j in range(group):
                total = row_weight(rate, span, place ^ j) * before
                for q in range(group):
                    if q != j:
                        total = total + row_weight(rate, span, (place ^ j) - 1 - (place ^ q)) * own[q]
                outs[j][start + i] = total.astype(BF16)


WHOLE = pl.BlockSpec(memory_space=pltpu.VMEM)
ANYWHERE = pl.BlockSpec(memory_space=pl.ANY)


def call(body, inputs, outputs, scratch=(), anywhere=(), out_anywhere=(), aliases=None, flops=0, name=None):
    nbytes = sum(a.size * a.dtype.itemsize for a in inputs) + sum(s.size * s.dtype.itemsize for s in outputs)
    return pl.pallas_call(
        body,
        in_specs=[ANYWHERE if n in anywhere else WHOLE for n in range(len(inputs))],
        out_specs=[ANYWHERE if n in out_anywhere else WHOLE for n in range(len(outputs))],
        scratch_shapes=list(scratch),
        out_shape=list(outputs),
        input_output_aliases=aliases or {},
        compiler_params=pltpu.CompilerParams(vmem_limit_bytes=VMEM_LIMIT),
        cost_estimate=pl.CostEstimate(flops=flops, bytes_accessed=nbytes, transcendentals=0),
        name=name,
    )(*inputs)


def level_sizes(devices):
    sizes = [2]
    left = devices // 2
    while left > 8:
        sizes.append(4)
        left //= 4
    return sizes + [left]


def swap(array, distance, devices):
    return lax.ppermute(array, AXES, [(i, i ^ distance) for i in range(devices)])


def carry_states(kept, sent, devices, rates, length, forward, beside):
    sizes = level_sizes(devices)
    state = kept.shape[1:]

    def climb(level, low, parts):
        group, next_group = sizes[level], sizes[level + 1]
        top = level + 2 == len(sizes)
        span = float(length * low)
        states = [parts[0]] + [swap(parts[k], k * low, devices) for k in range(1, group)]
        heads = parts[0].shape[0]
        count = 1 if top else next_group
        part_heads = heads if top else heads // next_group
        extra = list(beside[0]) if level == 1 else []
        inputs = [rates] + states + extra
        folded = call(
            functools.partial(fold_kernel, sizes, level, span, forward),
            inputs,
            [jax.ShapeDtypeStruct((part_heads,) + state, BF16)] * count,
            anywhere=range(1 + group, len(inputs)),
            name="fold_states",
        )
        if top:
            ahead = [swap(folded[0], k * low * group, devices) for k in range(1, next_group)]
        else:
            ahead = climb(level + 1, low * group, folded)
        extra = list(beside[1]) if level == 1 else []
        inputs = [rates] + states + ahead + extra
        outs = call(
            functools.partial(spread_kernel, sizes, level, span, forward),
            inputs,
            [jax.ShapeDtypeStruct((heads,) + state, BF16)] * group,
            anywhere=range(1 + group + len(ahead), len(inputs)),
            name="spread_states",
        )
        return [outs[0]] + [swap(outs[k], k * low, devices) for k in range(1, group)]

    return climb(0, 1, [kept, sent])


def local(devices, queries, key_vectors, value_vectors, output_grad, decay_rate, norm_gain):
    length, heads, size = queries.shape
    half = heads // 2
    rates = jnp.broadcast_to(decay_rate[:, None], (heads, size))

    def shaped(*shape, dtype=BF16):
        return jax.ShapeDtypeStruct(shape, dtype)

    per_head = shaped(half, length, size)
    per_head_wide = shaped(half, length, size, dtype=F32)
    states = shaped(half, size, size)
    whole = shaped(length, heads, size)
    flat = pltpu.VMEM((length * half, size), F32)
    stage = pltpu.VMEM((length, half, size), BF16)
    sems = pltpu.SemaphoreType.DMA((2, CHUNKS))
    unit = 2 * half * length * size * size

    keys, values, local_states = [None, None], [None, None], [None, None]
    for s in (1, 0):
        keys[s], values[s], local_states[s] = call(
            functools.partial(local_kernel, s == 0),
            [key_vectors, value_vectors, rates],
            [per_head, per_head, states],
            [stage, stage, flat, flat, sems],
            anywhere=(0, 1),
            flops=unit,
            name="local_states",
        )
    query, grad, attention, inner = [None, None], [None, None], [None, None], [None, None]
    for s in (0, 1):
        query[s], grad[s], attention[s], inner[s] = call(
            functools.partial(attention_kernel, s == 0),
            [queries, output_grad, keys[s], values[s], rates],
            [per_head, per_head, shaped(half, length, length), per_head_wide],
            [flat, flat],
            flops=2 * unit,
            name="attention",
        )
    incoming = carry_states(
        local_states[0], local_states[1], devices, rates, length, True, [inner[:1], inner[1:]]
    )
    normed, grad_out, state_grad = [None, None], [None, None], [None, None]
    for s in (0, 1):
        normed[s], grad_out[s], state_grad[s] = call(
            functools.partial(norm_kernel, s == 0),
            [query[s], grad[s], inner[s], incoming[s], rates, norm_gain],
            [per_head, per_head, states],
            flops=2 * unit,
            name="norm",
        )
    normed_out, query_out, key_part, value_part = None, None, [None, None], [None, None]
    for s in (0, 1):
        inputs = [query[s], keys[s], values[s], attention[s], grad_out[s], incoming[s], normed[s], rates]
        count = len(inputs)
        aliases = {}
        if s:
            aliases = {count: 0, count + 1: 1}
            inputs += [normed_out, query_out]
        normed_out, query_out, key_part[s], value_part[s] = call(
            functools.partial(grad_kernel, s == 0),
            inputs,
            [whole, whole, per_head_wide, per_head_wide],
            [flat, flat, stage, stage, sems],
            anywhere=(count, count + 1),
            out_anywhere=(0, 1),
            aliases=aliases,
            flops=5 * unit,
            name="stretch_gradients",
        )
    later = carry_states(
        state_grad[1], state_grad[0], devices, rates, length, False, [key_part[:1], key_part[1:]]
    )
    key_out, value_out = None, None
    for s in (1, 0):
        inputs = [keys[s], values[s], later[1 - s], key_part[s], value_part[s], rates]
        count = len(inputs)
        aliases = {}
        if s == 0:
            aliases = {count: 0, count + 1: 1}
            inputs += [key_out, value_out]
        key_out, value_out = call(
            functools.partial(later_kernel, s == 0),
            inputs,
            [whole, whole],
            [flat, flat, stage, stage, sems],
            anywhere=(count, count + 1),
            out_anywhere=(0, 1),
            aliases=aliases,
            flops=2 * unit,
            name="later_gradients",
        )
    return normed_out, query_out, key_out, value_out


def solution(mesh):
    devices = mesh.shape["ctx"] * mesh.shape["head"]
    spread = P(AXES, None, None)
    return jax.shard_map(
        functools.partial(local, devices),
        mesh=mesh,
        in_specs=(spread, spread, spread, spread, P(), P()),
        out_specs=(spread, spread, spread, spread),
        check_vma=False,
    )
```

```python
import functools
import jax
import jax.numpy as jnp
from jax import lax
from jax.experimental import pallas as pl
from jax.experimental.pallas import tpu as pltpu
from jax.sharding import PartitionSpec as P

AXES = ("ctx", "head")
F32 = jnp.float32
BF16 = jnp.bfloat16
VMEM_LIMIT = 16 * 1024 * 1024
LOCAL_LIMIT = 51 * 1024 * 1024
BATCH = 16
CHUNKS = 4
PIECES = 1
DOUBLING = True


def dot(a, b, dims):
    return lax.dot_general(a, b, (dims, ((), ())), preferred_element_type=F32)


AB = ((1,), (0,))
ABT = ((1,), (1,))
ATB = ((0,), (0,))


def decay(rate, steps):
    return jnp.exp(-rate * steps)


def positions(shape):
    return lax.broadcasted_iota(jnp.int32, shape, 0).astype(F32)


def causal_weights(rate, length):
    row = lax.broadcasted_iota(jnp.int32, (length, length), 0)
    col = lax.broadcasted_iota(jnp.int32, (length, length), 1)
    offset = (row - col).astype(F32)
    return jnp.where(offset >= 0, jnp.exp(-rate * jnp.maximum(offset, 0.0)), 0.0)


def my_index():
    return lax.axis_index("ctx") * lax.axis_size("head") + lax.axis_index("head")


def head_half(own):
    core = my_index() % 2
    return core if own else 1 - core


def split_heads(block_ref, scratch, half, heads):
    length, _, size = block_ref.shape
    start = pl.multiple_of(half * heads, heads)
    scratch[...] = block_ref[:, pl.ds(start, heads), :].astype(F32).reshape(length * heads, size)


def one_head(scratch, h, length, heads):
    return scratch[pl.ds(h, length, stride=heads), :]


def start_output(scratch, stage, out_ref, sems, half):
    length, heads, size = stage.shape
    chunks = sems.shape[0]
    rows = length // chunks
    start = pl.multiple_of(half * heads, heads)
    copies = []
    for c in range(chunks):
        piece = pl.ds(c * rows, rows)
        stage[piece] = scratch[pl.ds(c * rows * heads, rows * heads), :].reshape(rows, heads, size).astype(BF16)
        copy = pltpu.make_async_copy(stage.at[piece], out_ref.at[piece, pl.ds(start, heads), :], sems.at[c])
        copy.start()
        copies.append(copy)
    return copies


def batches(heads, size=BATCH):
    size = min(size, heads)
    return [range(start, start + size) for start in range(0, heads, size)]


def local_states(ks, vs, rates, kt_ref, vt_ref, s_ref):
    heads, length, size = kt_ref.shape
    tail_steps = length - 1.0 - positions((length, size))
    for batch in batches(heads):
        key = [one_head(ks, h, length, heads) for h in batch]
        value = [one_head(vs, h, length, heads).astype(BF16) for h in batch]
        tail = [decay(rates[h], tail_steps) for h in batch]
        decayed = [(k * t).astype(BF16) for k, t in zip(key, tail)]
        state = [dot(k, v, ATB) for k, v in zip(decayed, value)]
        for i, h in enumerate(batch):
            kt_ref[h] = key[i].astype(BF16)
            vt_ref[h] = value[i]
            s_ref[h] = state[i].astype(BF16)


def first_local_kernel(k_ref, v_ref, rates_ref, kt_ref, vt_ref, s_ref, k_rest, v_rest, rates_out, *scratch):
    kb, vb, ks, vs, rates, sems, rest_sems, rate_sem = scratch
    length, heads, size = kb.shape
    half = head_half(False)
    start = pl.multiple_of(half * heads, heads)
    rest = pl.multiple_of((1 - half) * heads, heads)
    chunks = sems.shape[1]
    rows = length // chunks
    rate_copy = pltpu.make_async_copy(rates_ref, rates, rate_sem)
    rate_copy.start()
    copies = []
    for c in range(chunks):
        piece = pl.ds(c * rows, rows)
        for n, (ref, buffer) in enumerate(((k_ref, kb), (v_ref, vb))):
            copy = pltpu.make_async_copy(ref.at[piece, pl.ds(start, heads), :], buffer.at[piece], sems.at[n, c])
            copy.start()
            copies.append(copy)
    rest_copies = []
    for n, (ref, buffer) in enumerate(((k_ref, k_rest), (v_ref, v_rest))):
        copy = pltpu.make_async_copy(ref.at[:, pl.ds(rest, heads), :], buffer, rest_sems.at[n])
        copy.start()
        rest_copies.append(copy)
    for c in range(chunks):
        piece = pl.ds(c * rows, rows)
        flat = pl.ds(c * rows * heads, rows * heads)
        copies[2 * c].wait()
        ks[flat, :] = kb[piece].astype(F32).reshape(rows * heads, size)
        copies[2 * c + 1].wait()
        vs[flat, :] = vb[piece].astype(F32).reshape(rows * heads, size)
    rate_copy.wait()
    for h in range(rates.shape[0]):
        rates_out[pl.ds(h, 1), :] = jnp.full((1, size), rates[h], F32)
    local_states(ks, vs, [rates[start + h] for h in range(heads)], kt_ref, vt_ref, s_ref)
    for copy in rest_copies:
        copy.wait()


def second_local_kernel(k_ref, v_ref, rate_ref, kt_ref, vt_ref, s_ref, ks, vs):
    heads, length, size = kt_ref.shape
    first = head_half(True) * heads
    ks[...] = k_ref[...].astype(F32).reshape(length * heads, size)
    vs[...] = v_ref[...].astype(F32).reshape(length * heads, size)
    rates = [rate_ref[pl.ds(first + h, 1), :] for h in range(heads)]
    local_states(ks, vs, rates, kt_ref, vt_ref, s_ref)


def attention_kernel(own, q_ref, g_ref, kt_ref, vt_ref, rate_ref, qt_ref, gt_ref, a_ref, o_ref, qs, gs):
    heads, length, size = kt_ref.shape
    half = head_half(own)
    first = half * heads
    split_heads(q_ref, qs, half, heads)
    split_heads(g_ref, gs, half, heads)
    for batch in batches(heads):
        query = [one_head(qs, h, length, heads).astype(BF16) for h in batch]
        scores = [dot(q, kt_ref[h], ABT) for q, h in zip(query, batch)]
        weights = [causal_weights(rate_ref[pl.ds(first + h, 1), :], length) for h in batch]
        attention = [(s * w).astype(BF16) for s, w in zip(scores, weights)]
        inner = [dot(a, vt_ref[h], AB) for a, h in zip(attention, batch)]
        for i, h in enumerate(batch):
            qt_ref[h] = query[i]
            gt_ref[h] = one_head(gs, h, length, heads).astype(BF16)
            a_ref[h] = attention[i]
            o_ref[h] = inner[i]


def norm_kernel(own, qt_ref, gt_ref, o_ref, in_ref, rate_ref, gain_ref, n_ref, go_ref, sg_ref):
    heads, length, size = qt_ref.shape
    first = head_half(own) * heads
    head_steps = positions((length, size)) + 1.0
    for batch in batches(heads):
        through = [dot(qt_ref[h], in_ref[h], AB) for h in batch]
        head_decay = [decay(rate_ref[pl.ds(first + h, 1), :], head_steps) for h in batch]
        out = [o_ref[h] + d * t for h, d, t in zip(batch, head_decay, through)]
        inv_rms = [lax.rsqrt(jnp.mean(o * o, axis=-1, keepdims=True) + 1e-06) for o in out]
        unit = [o * r for o, r in zip(out, inv_rms)]
        gain = [gain_ref[pl.ds(first + h, 1), :] for h in batch]
        scaled = [g * gt_ref[h].astype(F32) for g, h in zip(gain, batch)]
        along = [jnp.mean(s * u, axis=-1, keepdims=True) for s, u in zip(scaled, unit)]
        grad_out = [
            (r * (s - u * m)).astype(BF16) for r, s, u, m in zip(inv_rms, scaled, unit, along)
        ]
        decayed = [(qt_ref[h].astype(F32) * d).astype(BF16) for h, d in zip(batch, head_decay)]
        state = [dot(q, g, ATB) for q, g in zip(decayed, grad_out)]
        for i, h in enumerate(batch):
            n_ref[h] = (unit[i] * gain[i]).astype(BF16)
            go_ref[h] = grad_out[i]
            sg_ref[h] = state[i].astype(BF16)


def inner_kernel(own, qt_ref, vt_ref, a_ref, go_ref, rate_ref, gs_ref, dk_ref, dv_ref):
    heads, length, size = qt_ref.shape
    first = head_half(own) * heads
    for batch in batches(heads):
        inner = [dot(go_ref[h], vt_ref[h], ABT) for h in batch]
        value = [dot(a_ref[h], go_ref[h], ATB) for h in batch]
        weights = [causal_weights(rate_ref[pl.ds(first + h, 1), :], length) for h in batch]
        scores = [(s * w).astype(BF16) for s, w in zip(inner, weights)]
        key = [dot(s, qt_ref[h], ATB) for s, h in zip(scores, batch)]
        for i, h in enumerate(batch):
            gs_ref[h] = scores[i]
            dv_ref[h] = value[i]
            dk_ref[h] = key[i]


def query_kernel(own, kt_ref, gs_ref, go_ref, in_ref, n_ref, rate_ref, *rest):
    n_out, dq_out, mark_ref, ns, ds, nb, db, sems = rest[-8:]
    mark_ref[...] = jnp.zeros(mark_ref.shape, F32)
    heads, length, size = kt_ref.shape
    half = head_half(own)
    first = half * heads
    head_steps = positions((length, size)) + 1.0
    for h in range(heads):
        ns[pl.ds(h, length, stride=heads), :] = n_ref[h].astype(F32)
    copies = start_output(ns, nb, n_out, sems.at[0], half)
    for batch in batches(heads):
        through = [dot(go_ref[h], in_ref[h], ABT) for h in batch]
        query = [dot(gs_ref[h], kt_ref[h], AB) for h in batch]
        for i, h in enumerate(batch):
            head_decay = decay(rate_ref[pl.ds(first + h, 1), :], head_steps)
            ds[pl.ds(h, length, stride=heads), :] = query[i] + head_decay * through[i]
    copies += start_output(ds, db, dq_out, sems.at[1], half)
    for copy in copies:
        copy.wait()


def later_kernel(own, kt_ref, vt_ref, later_ref, dk_ref, dv_ref, rate_ref, *rest):
    dk_out, dv_out, ks, vs, kb, vb, sems = rest[-7:]
    heads, length, size = kt_ref.shape
    half = head_half(own)
    first = half * heads
    tail_steps = length - 1.0 - positions((length, size))
    for batch in batches(heads):
        key = [dot(vt_ref[h], later_ref[h], ABT) for h in batch]
        value = [dot(kt_ref[h], later_ref[h], AB) for h in batch]
        for i, h in enumerate(batch):
            tail = decay(rate_ref[pl.ds(first + h, 1), :], tail_steps)
            ks[pl.ds(h, length, stride=heads), :] = dk_ref[h] + tail * key[i]
            vs[pl.ds(h, length, stride=heads), :] = dv_ref[h] + tail * value[i]
    copies = start_output(ks, kb, dk_out, sems.at[0], half)
    copies += start_output(vs, vb, dv_out, sems.at[1], half)
    for copy in copies:
        copy.wait()


def row_weight(rate, span, steps):
    weight = jnp.exp(-rate * (span * jnp.maximum(steps, 0).astype(F32)))
    return jnp.where(steps >= 0, weight, 0.0)


def place_at(sizes, level, forward=True):
    low = 1
    for size in sizes[:level]:
        low *= size
    place = (my_index() // low) % sizes[level]
    return place if forward else place ^ (sizes[level] - 1)


def first_head(sizes, level, heads, forward):
    first, count = 0, heads
    for above in range(level + 1):
        count //= sizes[above]
        place = place_at(sizes, above)
        if above == 0 and not forward:
            place = 1 - place
        first = first + place * count
    return first


def fold_kernel(sizes, level, shift, pieces, span, forward, rate_ref, *refs):
    group = sizes[level]
    top = level + 2 == len(sizes)
    count = 1 if top else sizes[level + 1]
    states, parts = refs[:group], refs[len(refs) - count * pieces :]
    heads = parts[0].shape[0]
    first = first_head(sizes, level, rate_ref.shape[0], forward) + shift
    place = place_at(sizes, level, forward)
    weigh = [group - 1 - (place ^ j) for j in range(group)]
    for k in range(count):
        part = 0 if top else place_at(sizes, level + 1) ^ k
        for g in range(pieces):
            start = (part * pieces + g) * heads
            for i in range(heads):
                rate = rate_ref[pl.ds(first + start + i, 1), :]
                total = None
                for j in range(group):
                    term = row_weight(rate, span, weigh[j]) * states[j][start + i].astype(F32)
                    total = term if total is None else total + term
                parts[g * count + k][i] = total.astype(BF16)


def double_kernel(sizes, level, shift, step, span, forward, rate_ref, state_ref, other_ref, *rest):
    out_ref = rest[-1]
    first = first_head(sizes, level - 1, rate_ref.shape[0], forward) + shift
    upper = (place_at(sizes, level, forward) // step) % 2
    for i in range(out_ref.shape[0]):
        rate = rate_ref[pl.ds(first + i, 1), :]
        total = row_weight(rate, span * step, 1 - upper) * state_ref[i].astype(F32)
        total = total + row_weight(rate, span * step, upper) * other_ref[i].astype(F32)
        out_ref[i] = total.astype(BF16)


def spread_kernel(sizes, level, shift, pieces, span, forward, rate_ref, *refs):
    group, next_group = sizes[level], sizes[level + 1]
    top = level + 2 == len(sizes)
    count = 1 if top else next_group
    ahead_count = next_group * pieces
    if top:
        ahead_count = next_group.bit_length() - 1 if DOUBLING else next_group - 1
    states, ahead, outs = refs[:group], refs[group : group + ahead_count], refs[len(refs) - group :]
    heads = states[0].shape[0]
    part_heads = heads if top else heads // (next_group * pieces)
    first = first_head(sizes, level, rate_ref.shape[0], forward) + shift
    place = place_at(sizes, level, forward)
    top_place = place_at(sizes, level + 1, forward)
    for k in range(count):
        part = 0 if top else place_at(sizes, level + 1) ^ k
        for g in range(pieces):
            start = (part * pieces + g) * part_heads
            for i in range(part_heads):
                rate = rate_ref[pl.ds(first + start + i, 1), :]
                if top:
                    before = None
                    for j in range(ahead_count):
                        steps = top_place - 1 - (top_place ^ (j + 1))
                        if DOUBLING:
                            step = 1 << j
                            steps = jnp.where((top_place // step) % 2 == 1, top_place % step, -1)
                        term = row_weight(rate, span * group, steps) * ahead[j][i].astype(F32)
                        before = term if before is None else before + term
                else:
                    before = ahead[g * count + k][i].astype(F32)
                own = [states[j][start + i].astype(F32) for j in range(group)]
                for j in range(group):
                    total = row_weight(rate, span, place ^ j) * before
                    for q in range(group):
                        if q != j:
                            total = total + row_weight(rate, span, (place ^ j) - 1 - (place ^ q)) * own[q]
                    outs[j][start + i] = total.astype(BF16)


WHOLE = pl.BlockSpec(memory_space=pltpu.VMEM)
ANYWHERE = pl.BlockSpec(memory_space=pl.ANY)
OUTSIDE = pl.BlockSpec(memory_space=pltpu.HBM)


def call(body, inputs, outputs, scratch=(), anywhere=(), outside=(), out_outside=(), aliases=None, flops=0, name=None, limit=VMEM_LIMIT, count_bytes=True):
    nbytes = sum(a.size * a.dtype.itemsize for a in inputs) + sum(s.size * s.dtype.itemsize for s in outputs)
    nbytes = nbytes if count_bytes else 0
    return pl.pallas_call(
        body,
        in_specs=[ANYWHERE if n in anywhere else OUTSIDE if n in outside else WHOLE for n in range(len(inputs))],
        out_specs=[OUTSIDE if n in out_outside else WHOLE for n in range(len(outputs))],
        scratch_shapes=list(scratch),
        out_shape=list(outputs),
        input_output_aliases=aliases or {},
        compiler_params=pltpu.CompilerParams(vmem_limit_bytes=limit),
        cost_estimate=pl.CostEstimate(flops=flops, bytes_accessed=nbytes, transcendentals=0),
        name=name,
    )(*inputs)


def level_sizes(devices):
    sizes = [2]
    left = devices // 2
    while left > 8:
        sizes.append(4)
        left //= 4
    return sizes + [left]


def swap(array, distance, devices):
    return lax.ppermute(array, AXES, [(i, i ^ distance) for i in range(devices)])


def carry_states(kept, sent, devices, rates, length, forward, beside):
    sizes = level_sizes(devices)
    state = kept.shape[1:]
    left = kept.shape[0]
    for size in sizes[1:-1]:
        left //= size
    pieces = min(PIECES, left) if len(sizes) > 2 else 1

    def climb(level, low, parts, shift, piece):
        group, next_group = sizes[level], sizes[level + 1]
        top = level + 2 == len(sizes)
        cut = pieces if level == 0 else 1
        span = float(length * low)
        states = [parts[0]] + [swap(parts[k], k * low, devices) for k in range(1, group)]
        heads = parts[0].shape[0]
        count = 1 if top else next_group
        part_heads = heads if top else heads // (next_group * cut)
        extra = list(beside.get(("fold", piece), ())) if level == 1 else []
        inputs = [rates] + states + extra
        folded = call(
            functools.partial(fold_kernel, sizes, level, shift, cut, span, forward),
            inputs,
            [jax.ShapeDtypeStruct((part_heads,) + state, BF16)] * (count * cut),
            anywhere=range(1 + group, len(inputs)),
            name="fold_states",
        )
        if top and not DOUBLING:
            ahead = [swap(folded[0], k * low * group, devices) for k in range(1, next_group)]
        elif top:
            total, ahead, step = folded[0], [], 1
            while step < next_group:
                if step > 1:
                    extra = list(beside.get(("double", piece), ()))
                    inputs = [rates, total, ahead[-1]] + extra
                    (total,) = call(
                        functools.partial(
                            double_kernel, sizes, level + 1, shift, step // 2, span * group, forward
                        ),
                        inputs,
                        [jax.ShapeDtypeStruct((part_heads,) + state, BF16)],
                        anywhere=range(3, len(inputs)),
                        name="double_states",
                    )
                ahead.append(swap(total, step * low * group, devices))
                step *= 2
        else:
            ahead = []
            for g in range(cut):
                ahead += climb(
                    level + 1, low * group, folded[g * count : (g + 1) * count], shift + g * part_heads, g
                )
        extra = list(beside.get(("spread", piece if level else -1), ())) if level < 2 else []
        inputs = [rates] + states + ahead + extra
        outs = call(
            functools.partial(spread_kernel, sizes, level, shift, cut, span, forward),
            inputs,
            [jax.ShapeDtypeStruct((heads,) + state, BF16)] * group,
            anywhere=range(1 + group + len(ahead), len(inputs)),
            name="spread_states",
        )
        return [outs[0]] + [swap(outs[k], k * low, devices) for k in range(1, group)]

    return climb(0, 1, [kept, sent], 0, 0)


def local(devices, queries, key_vectors, value_vectors, output_grad, decay_rate, norm_gain):
    length, heads, size = queries.shape
    half = heads // 2

    def shaped(*shape, dtype=BF16):
        return jax.ShapeDtypeStruct(shape, dtype)

    per_head = shaped(half, length, size)
    per_head_wide = shaped(half, length, size, dtype=F32)
    states = shaped(half, size, size)
    whole = shaped(length, heads, size)
    flat = pltpu.VMEM((length * half, size), F32)
    stage = pltpu.VMEM((length, half, size), BF16)
    sems = pltpu.SemaphoreType.DMA((2, CHUNKS))
    unit = 2 * half * length * size * size

    rate_rows = shaped(heads, size, dtype=F32)
    block = shaped(length, half, size)
    copy_sem = pltpu.SemaphoreType.DMA
    sent_key, sent_value, sent_state, key_rest, value_rest, rates = call(
        first_local_kernel,
        [key_vectors, value_vectors, decay_rate],
        [per_head, per_head, states, block, block, rate_rows],
        [stage, stage, flat, flat, pltpu.SMEM((heads,), F32), sems, copy_sem((2,)), copy_sem],
        outside=(0, 1, 2),
        limit=LOCAL_LIMIT,
        count_bytes=False,
        flops=unit,
        name="local_states",
    )
    kept_key, kept_value, kept_state = call(
        second_local_kernel,
        [key_rest, value_rest, rates],
        [per_head, per_head, states],
        [flat, flat],
        flops=unit,
        name="local_states",
    )
    keys, values = [kept_key, sent_key], [kept_value, sent_value]
    query, grad, attention, inner = [None, None], [None, None], [None, None], [None, None]
    for s in (0, 1):
        query[s], grad[s], attention[s], inner[s] = call(
            functools.partial(attention_kernel, s == 0),
            [queries, output_grad, keys[s], values[s], rates],
            [per_head, per_head, shaped(half, length, length), per_head_wide],
            [flat, flat],
            flops=2 * unit,
            name="attention",
        )
    incoming = carry_states(
        kept_state, sent_state, devices, rates, length, True, {("fold", 0): inner[:1], ("spread", 0): inner[1:]}
    )
    normed, grad_out, state_grad = [None, None], [None, None], [None, None]
    for s in (0, 1):
        normed[s], grad_out[s], state_grad[s] = call(
            functools.partial(norm_kernel, s == 0),
            [query[s], grad[s], inner[s], incoming[s], rates, norm_gain],
            [per_head, per_head, states],
            flops=2 * unit,
            name="norm",
        )
    normed_out, query_out = None, None
    scores, key_part, value_part, marks = [None, None], [None, None], [None, None], []
    for s in (0, 1):
        scores[s], key_part[s], value_part[s] = call(
            functools.partial(inner_kernel, s == 0),
            [query[s], values[s], attention[s], grad_out[s], rates],
            [shaped(half, length, length), per_head_wide, per_head_wide],
            flops=3 * unit,
            name="inner_gradients",
        )
        inputs = [keys[s], scores[s], grad_out[s], incoming[s], normed[s], rates]
        count = len(inputs)
        aliases = {}
        if s:
            aliases = {count: 0, count + 1: 1}
            inputs += [normed_out, query_out]
        normed_out, query_out, mark = call(
            functools.partial(query_kernel, s == 0),
            inputs,
            [whole, whole, shaped(8, size, dtype=F32)],
            [flat, flat, stage, stage, sems],
            outside=(count, count + 1),
            out_outside=(0, 1),
            aliases=aliases,
            flops=2 * unit,
            name="query_gradient",
        )
        marks += [key_part[s], mark]
    later = carry_states(
        state_grad[1], state_grad[0], devices, rates, length, False,
        {("fold", 0): marks[:1] + marks[2:3], ("spread", 0): marks[1:2], ("spread", -1): marks[3:]},

    )
    key_out, value_out = None, None
    for s in (1, 0):
        inputs = [keys[s], values[s], later[1 - s], key_part[s], value_part[s], rates]
        count = len(inputs)
        aliases = {}
        if s == 0:
            aliases = {count: 0, count + 1: 1}
            inputs += [key_out, value_out]
        key_out, value_out = call(
            functools.partial(later_kernel, s == 0),
            inputs,
            [whole, whole],
            [flat, flat, stage, stage, sems],
            outside=(count, count + 1),
            out_outside=(0, 1),
            aliases=aliases,
            flops=2 * unit,
            name="later_gradients",
        )
    return normed_out, query_out, key_out, value_out


def solution(mesh):
    devices = mesh.shape["ctx"] * mesh.shape["head"]
    spread = P(AXES, None, None)
    return jax.shard_map(
        functools.partial(local, devices),
        mesh=mesh,
        in_specs=(spread, spread, spread, spread, P(), P()),
        out_specs=(spread, spread, spread, spread),
        check_vma=False,
    )
```

```python
import functools
import jax
import jax.numpy as jnp
from jax import lax
from jax.experimental import pallas as pl
from jax.experimental.pallas import tpu as pltpu
from jax.sharding import PartitionSpec as P

AXES = ("ctx", "head")
F32 = jnp.float32
BF16 = jnp.bfloat16
VMEM_LIMIT = 16 * 1024 * 1024
LOCAL_LIMIT = 51 * 1024 * 1024
BATCH = 16
CHUNKS = 4


def dot(a, b, dims):
    return lax.dot_general(a, b, (dims, ((), ())), preferred_element_type=F32)


AB = ((1,), (0,))
ABT = ((1,), (1,))
ATB = ((0,), (0,))


def decay(rate, steps):
    return jnp.exp(-rate * steps)


def positions(shape):
    return lax.broadcasted_iota(jnp.int32, shape, 0).astype(F32)


def causal_weights(rate, length):
    row = lax.broadcasted_iota(jnp.int32, (length, length), 0)
    col = lax.broadcasted_iota(jnp.int32, (length, length), 1)
    offset = (row - col).astype(F32)
    return jnp.where(offset >= 0, jnp.exp(-rate * jnp.maximum(offset, 0.0)), 0.0)


def my_index():
    return lax.axis_index("ctx") * lax.axis_size("head") + lax.axis_index("head")


def head_half(own):
    core = my_index() % 2
    return core if own else 1 - core


def split_heads(block_ref, scratch, half, heads):
    length, _, size = block_ref.shape
    start = pl.multiple_of(half * heads, heads)
    scratch[...] = block_ref[:, pl.ds(start, heads), :].astype(F32).reshape(length * heads, size)


def one_head(scratch, h, length, heads):
    return scratch[pl.ds(h, length, stride=heads), :]


def start_output(scratch, stage, out_ref, sems, half):
    length, heads, size = stage.shape
    chunks = sems.shape[0]
    rows = length // chunks
    start = pl.multiple_of(half * heads, heads)
    copies = []
    for c in range(chunks):
        piece = pl.ds(c * rows, rows)
        stage[piece] = scratch[pl.ds(c * rows * heads, rows * heads), :].reshape(rows, heads, size).astype(BF16)
        copy = pltpu.make_async_copy(stage.at[piece], out_ref.at[piece, pl.ds(start, heads), :], sems.at[c])
        copy.start()
        copies.append(copy)
    return copies


def batches(heads, size=BATCH):
    size = min(size, heads)
    return [range(start, start + size) for start in range(0, heads, size)]


def local_states(ks, vs, rates, kt_ref, vt_ref, s_ref):
    heads, length, size = kt_ref.shape
    tail_steps = length - 1.0 - positions((length, size))
    for batch in batches(heads):
        key = [one_head(ks, h, length, heads) for h in batch]
        value = [one_head(vs, h, length, heads).astype(BF16) for h in batch]
        tail = [decay(rates[h], tail_steps) for h in batch]
        decayed = [(k * t).astype(BF16) for k, t in zip(key, tail)]
        state = [dot(k, v, ATB) for k, v in zip(decayed, value)]
        for i, h in enumerate(batch):
            kt_ref[h] = key[i].astype(BF16)
            vt_ref[h] = value[i]
            s_ref[h] = state[i].astype(BF16)


def first_local_kernel(k_ref, v_ref, rates_ref, kt_ref, vt_ref, s_ref, k_rest, v_rest, rates_out, *scratch):
    kb, vb, ks, vs, rates, sems, rest_sems, rate_sem = scratch
    length, heads, size = kb.shape
    half = head_half(False)
    start = pl.multiple_of(half * heads, heads)
    rest = pl.multiple_of((1 - half) * heads, heads)
    chunks = sems.shape[1]
    rows = length // chunks
    rate_copy = pltpu.make_async_copy(rates_ref, rates, rate_sem)
    rate_copy.start()
    copies = []
    for c in range(chunks):
        piece = pl.ds(c * rows, rows)
        for n, (ref, buffer) in enumerate(((k_ref, kb), (v_ref, vb))):
            copy = pltpu.make_async_copy(ref.at[piece, pl.ds(start, heads), :], buffer.at[piece], sems.at[n, c])
            copy.start()
            copies.append(copy)
    rest_copies = []
    for n, (ref, buffer) in enumerate(((k_ref, k_rest), (v_ref, v_rest))):
        copy = pltpu.make_async_copy(ref.at[:, pl.ds(rest, heads), :], buffer, rest_sems.at[n])
        copy.start()
        rest_copies.append(copy)
    for c in range(chunks):
        piece = pl.ds(c * rows, rows)
        flat = pl.ds(c * rows * heads, rows * heads)
        copies[2 * c].wait()
        ks[flat, :] = kb[piece].astype(F32).reshape(rows * heads, size)
        copies[2 * c + 1].wait()
        vs[flat, :] = vb[piece].astype(F32).reshape(rows * heads, size)
    rate_copy.wait()
    for h in range(rates.shape[0]):
        rates_out[pl.ds(h, 1), :] = jnp.full((1, size), rates[h], F32)
    local_states(ks, vs, [rates[start + h] for h in range(heads)], kt_ref, vt_ref, s_ref)
    for copy in rest_copies:
        copy.wait()


def second_local_kernel(k_ref, v_ref, rate_ref, kt_ref, vt_ref, s_ref, ks, vs):
    heads, length, size = kt_ref.shape
    first = head_half(True) * heads
    ks[...] = k_ref[...].astype(F32).reshape(length * heads, size)
    vs[...] = v_ref[...].astype(F32).reshape(length * heads, size)
    rates = [rate_ref[pl.ds(first + h, 1), :] for h in range(heads)]
    local_states(ks, vs, rates, kt_ref, vt_ref, s_ref)


def attention_kernel(own, q_ref, g_ref, kt_ref, vt_ref, rate_ref, gain_ref, *rest):
    qt_ref, qd_ref, qd_across_ref, scaled_ref, a_ref, o_ref, gain_out, qs, gs = rest
    gain_out[...] = gain_ref[...]
    heads, length, size = kt_ref.shape
    half = head_half(own)
    first = half * heads
    split_heads(q_ref, qs, half, heads)
    split_heads(g_ref, gs, half, heads)
    head_steps = positions((length, size)) + 1.0
    for batch in batches(heads):
        rate = [rate_ref[pl.ds(first + h, 1), :] for h in batch]
        wide = [one_head(qs, h, length, heads) for h in batch]
        query = [q.astype(BF16) for q in wide]
        decayed = [(q * decay(r, head_steps)).astype(BF16) for q, r in zip(wide, rate)]
        scores = [dot(q, kt_ref[h], ABT) for q, h in zip(query, batch)]
        weights = [causal_weights(r, length) for r in rate]
        attention = [(s * w).astype(BF16) for s, w in zip(scores, weights)]
        inner = [dot(a, vt_ref[h], AB) for a, h in zip(attention, batch)]
        for i, h in enumerate(batch):
            qt_ref[h] = query[i]
            qd_ref[h] = decayed[i]
            qd_across_ref[h] = decayed[i].T
            scaled_ref[h] = gain_ref[pl.ds(first + h, 1), :] * one_head(gs, h, length, heads)
            a_ref[h] = attention[i]
            o_ref[h] = inner[i]


def norm_kernel(own, sizes, ks, qd_ref, qd_across_ref, scaled_ref, o_ref, in_ref, gain_ref, *rest):
    n_ref, go_ref, all_in_ref, sg_ref = rest[-4:]
    first = head_half(own) * qd_ref.shape[0]
    places = part_heads_of(sizes, ks, in_ref.shape[0])
    for batch in batches(len(places)):
        out = [o_ref[places[h]] + dot(qd_ref[places[h]], in_ref[h], AB) for h in batch]
        inv_rms = [lax.rsqrt(jnp.mean(o * o, axis=-1, keepdims=True) + 1e-06) for o in out]
        unit = [o * r for o, r in zip(out, inv_rms)]
        gain = [gain_ref[pl.ds(first + places[h], 1), :] for h in batch]
        scaled = [scaled_ref[places[h]] for h in batch]
        along = [jnp.mean(s * u, axis=-1, keepdims=True) for s, u in zip(scaled, unit)]
        grad_out = [
            (r * (s - u * m)).astype(BF16) for r, s, u, m in zip(inv_rms, scaled, unit, along)
        ]
        state = [dot(qd_across_ref[places[h]], g, AB) for h, g in zip(batch, grad_out)]
        for i, h in enumerate(batch):
            n_ref[places[h]] = (unit[i] * gain[i]).astype(BF16)
            go_ref[places[h]] = grad_out[i]
            all_in_ref[places[h]] = in_ref[h]
            sg_ref[h] = state[i].astype(BF16)


def inner_kernel(own, qt_ref, kt_ref, vt_ref, a_ref, go_ref, rate_ref, gs_ref, dk_ref, dv_ref, kd_ref, vd_ref):
    heads, length, size = qt_ref.shape
    tail_steps = length - 1.0 - positions((length, size))
    first = head_half(own) * heads
    for batch in batches(heads):
        inner = [dot(go_ref[h], vt_ref[h], ABT) for h in batch]
        value = [dot(a_ref[h], go_ref[h], ATB) for h in batch]
        weights = [causal_weights(rate_ref[pl.ds(first + h, 1), :], length) for h in batch]
        scores = [(s * w).astype(BF16) for s, w in zip(inner, weights)]
        key = [dot(s, qt_ref[h], ATB) for s, h in zip(scores, batch)]
        for i, h in enumerate(batch):
            gs_ref[h] = scores[i]
            dv_ref[h] = value[i]
            dk_ref[h] = key[i]
            tail = decay(rate_ref[pl.ds(first + h, 1), :], tail_steps)
            kd_ref[h] = (kt_ref[h].astype(F32) * tail).astype(BF16)
            vd_ref[h] = (vt_ref[h].astype(F32) * tail).astype(BF16)


def query_kernel(own, kt_ref, gs_ref, go_ref, in_ref, n_ref, rate_ref, *rest):
    n_out, dq_out, mark_ref, ns, ds, nb, db, sems = rest[-8:]
    mark_ref[...] = jnp.zeros(mark_ref.shape, F32)
    heads, length, size = kt_ref.shape
    half = head_half(own)
    first = half * heads
    head_steps = positions((length, size)) + 1.0
    for h in range(heads):
        ns[pl.ds(h, length, stride=heads), :] = n_ref[h].astype(F32)
    copies = start_output(ns, nb, n_out, sems.at[0], half)
    for batch in batches(heads):
        through = [dot(go_ref[h], in_ref[h], ABT) for h in batch]
        query = [dot(gs_ref[h], kt_ref[h], AB) for h in batch]
        for i, h in enumerate(batch):
            head_decay = decay(rate_ref[pl.ds(first + h, 1), :], head_steps)
            ds[pl.ds(h, length, stride=heads), :] = query[i] + head_decay * through[i]
    copies += start_output(ds, db, dq_out, sems.at[1], half)
    for copy in copies:
        copy.wait()


def add_later(sizes, ks, kd_ref, vd_ref, later_ref, dk_ref, dv_ref, keys, values):
    heads, length, size = kd_ref.shape
    places = part_heads_of(sizes, ks, later_ref.shape[0])
    for batch in batches(len(places)):
        key = [dot(vd_ref[places[h]], later_ref[h], ABT) for h in batch]
        value = [dot(kd_ref[places[h]], later_ref[h], AB) for h in batch]
        for i, h in enumerate(batch):
            at = places[h]
            keys[pl.ds(at, length, stride=heads), :] = dk_ref[at] + key[i]
            values[pl.ds(at, length, stride=heads), :] = dv_ref[at] + value[i]


def later_kernel(sizes, ks, *refs):
    add_later(sizes, ks, *refs[:5], *refs[-2:])


def join_kernel(ks, vs, k_ref, v_ref):
    k_ref[...] = ks[...].reshape(k_ref.shape).astype(BF16)
    v_ref[...] = vs[...].reshape(v_ref.shape).astype(BF16)


def last_kernel(own, sizes, parts, *refs):
    k_rest, v_rest = refs[5:7]
    dk_out, dv_out, ks, vs, kb, vb, sems = refs[-7:]
    heads = kb.shape[1]
    half = head_half(own)
    start = pl.multiple_of((1 - half) * heads, heads)
    copies = []
    for n, (block, out) in enumerate(((k_rest, dk_out), (v_rest, dv_out))):
        copy = pltpu.make_async_copy(block, out.at[:, pl.ds(start, heads), :], sems.at[2, n])
        copy.start()
        copies.append(copy)
    add_later(sizes, parts, *refs[:5], ks, vs)
    copies += start_output(ks, kb, dk_out, sems.at[0], half)
    copies += start_output(vs, vb, dv_out, sems.at[1], half)
    for copy in copies:
        copy.wait()


def row_weight(rate, span, steps):
    weight = jnp.exp(-rate * (span * jnp.maximum(steps, 0).astype(F32)))
    return jnp.where(steps >= 0, weight, 0.0)


def place_at(sizes, level, forward=True):
    low = 1
    for size in sizes[:level]:
        low *= size
    place = (my_index() // low) % sizes[level]
    return place if forward else place ^ (sizes[level] - 1)


def first_head(sizes, level, heads, forward):
    first, count = 0, heads
    for above in range(level + 1):
        count //= sizes[above]
        place = place_at(sizes, above)
        if above == 0 and not forward:
            place = 1 - place
        first = first + place * count
    return first


def part_start(sizes, k, heads):
    return (place_at(sizes, 1) ^ k) * heads


def part_heads_of(sizes, ks, count):
    part = count // len(ks)
    return [part_start(sizes, k, part) + i for k in ks for i in range(part)]


def fold_kernel(sizes, level, span, forward, rate_ref, *refs):
    group = sizes[level]
    top = level + 2 == len(sizes)
    count = 1 if top else sizes[level + 1]
    states, parts = refs[:group], refs[len(refs) - count :]
    heads = parts[0].shape[0]
    first = first_head(sizes, level, rate_ref.shape[0], forward)
    place = place_at(sizes, level, forward)
    weigh = [group - 1 - (place ^ j) for j in range(group)]
    for k in range(count):
        start = 0 if top else (place_at(sizes, level + 1) ^ k) * heads
        for i in range(heads):
            rate = rate_ref[pl.ds(first + start + i, 1), :]
            total = None
            for j in range(group):
                term = row_weight(rate, span, weigh[j]) * states[j][start + i].astype(F32)
                total = term if total is None else total + term
            parts[k][i] = total.astype(BF16)


def pair_fold_kernel(sizes, ks, span, forward, rate_ref, kept_ref, other_ref, *rest):
    out_refs = rest[len(rest) - len(ks) :]
    first = first_head(sizes, 0, rate_ref.shape[0], forward)
    place = place_at(sizes, 0, forward)
    part = out_refs[0].shape[0]
    for i, head in enumerate(part_heads_of(sizes, ks, part * len(ks))):
        at = head if kept_ref.shape[0] > part * len(ks) else i
        rate = rate_ref[pl.ds(first + head, 1), :]
        total = row_weight(rate, span, 1 - place) * kept_ref[at].astype(F32)
        total = total + row_weight(rate, span, place) * other_ref[at].astype(F32)
        out_refs[i // part][i % part] = total.astype(BF16)


def double_kernel(sizes, level, step, span, forward, rate_ref, state_ref, other_ref, *rest):
    out_ref = rest[-1]
    first = first_head(sizes, level - 1, rate_ref.shape[0], forward)
    upper = (place_at(sizes, level, forward) // step) % 2
    for i in range(out_ref.shape[0]):
        rate = rate_ref[pl.ds(first + i, 1), :]
        total = row_weight(rate, span * step, 1 - upper) * state_ref[i].astype(F32)
        total = total + row_weight(rate, span * step, upper) * other_ref[i].astype(F32)
        out_ref[i] = total.astype(BF16)


def spread_kernel(sizes, level, span, forward, rate_ref, *refs):
    group, next_group = sizes[level], sizes[level + 1]
    top = level + 2 == len(sizes)
    count = 1 if top else next_group
    ahead_count = next_group.bit_length() - 1 if top else next_group
    states, ahead, outs = refs[:group], refs[group : group + ahead_count], refs[len(refs) - group :]
    heads = states[0].shape[0]
    part_heads = heads // count
    first = first_head(sizes, level, rate_ref.shape[0], forward)
    place = place_at(sizes, level, forward)
    top_place = place_at(sizes, level + 1, forward)
    for k in range(count):
        start = 0 if top else (place_at(sizes, level + 1) ^ k) * part_heads
        for i in range(part_heads):
            rate = rate_ref[pl.ds(first + start + i, 1), :]
            if top:
                before = None
                for j in range(ahead_count):
                    step = 1 << j
                    steps = jnp.where((top_place // step) % 2 == 1, top_place % step, -1)
                    term = row_weight(rate, span * group, steps) * ahead[j][i].astype(F32)
                    before = term if before is None else before + term
            else:
                before = ahead[k][i].astype(F32)
            own = [states[j][start + i].astype(F32) for j in range(group)]
            for j in range(group):
                total = row_weight(rate, span, place ^ j) * before
                for q in range(group):
                    if q != j:
                        total = total + row_weight(rate, span, (place ^ j) - 1 - (place ^ q)) * own[q]
                outs[j][start + i] = total.astype(BF16)


def pair_spread_kernel(sizes, ks, span, forward, rate_ref, kept_ref, other_ref, *rest):
    before_refs, (send_ref, mine_ref) = rest[: len(ks)], rest[-2:]
    count = send_ref.shape[0]
    part = count // len(ks)
    first = first_head(sizes, 0, rate_ref.shape[0], forward)
    place = place_at(sizes, 0, forward)
    for i, head in enumerate(part_heads_of(sizes, ks, count)):
        at = head if kept_ref.shape[0] > count else i
        rate = rate_ref[pl.ds(first + head, 1), :]
        before = before_refs[i // part][i % part].astype(F32)
        onward = row_weight(rate, span, 1) * before
        send = onward + kept_ref[at].astype(F32)
        send_ref[i] = jnp.where(place == 0, send, before).astype(BF16)
        mine = onward + other_ref[at].astype(F32)
        mine_ref[i] = jnp.where(place == 0, before, mine).astype(BF16)


WHOLE = pl.BlockSpec(memory_space=pltpu.VMEM)
ANYWHERE = pl.BlockSpec(memory_space=pl.ANY)
OUTSIDE = pl.BlockSpec(memory_space=pltpu.HBM)


def call(body, inputs, outputs, scratch=(), anywhere=(), outside=(), out_outside=(), aliases=None, flops=0, name=None, limit=VMEM_LIMIT, count_bytes=True):
    nbytes = sum(a.size * a.dtype.itemsize for a in inputs) + sum(s.size * s.dtype.itemsize for s in outputs)
    nbytes = nbytes if count_bytes else 0
    return list(pl.pallas_call(
        body,
        in_specs=[ANYWHERE if n in anywhere else OUTSIDE if n in outside else WHOLE for n in range(len(inputs))],
        out_specs=[OUTSIDE if n in out_outside else WHOLE for n in range(len(outputs))],
        scratch_shapes=list(scratch),
        out_shape=list(outputs),
        input_output_aliases=aliases or {},
        compiler_params=pltpu.CompilerParams(vmem_limit_bytes=limit),
        cost_estimate=pl.CostEstimate(flops=flops, bytes_accessed=nbytes, transcendentals=0),
        name=name,
    )(*inputs))


def level_sizes(devices):
    sizes = [2]
    left = devices // 2
    while left > 8:
        sizes.append(4)
        left //= 4
    return sizes + [left]


def swap(array, distance, devices):
    return lax.ppermute(array, AXES, [(i, i ^ distance) for i in range(devices)])


def carry_states(parts, sizes, devices, rates, length, forward, beside):
    state = parts[0].shape[1:]

    def climb(level, low, parts):
        group, next_group = sizes[level], sizes[level + 1]
        top = level + 2 == len(sizes)
        span = float(length * low)
        states = [parts[0]] + [swap(parts[k], k * low, devices) for k in range(1, group)]
        heads = parts[0].shape[0]
        count = 1 if top else next_group
        part = jax.ShapeDtypeStruct((heads // count,) + state, BF16)
        inputs = [rates] + states + (beside["fold"] if level == 1 else [])
        folded = call(
            functools.partial(fold_kernel, sizes, level, span, forward),
            inputs,
            [part] * count,
            anywhere=range(1 + group, len(inputs)),
            name="fold_states",
        )
        if top:
            total, ahead, step = folded[0], [], 1
            while step < next_group:
                if step > 1:
                    inputs = [rates, total, ahead[-1]] + (beside["double"] if step == 2 else [])
                    (total,) = call(
                        functools.partial(
                            double_kernel, sizes, level + 1, step // 2, span * group, forward
                        ),
                        inputs,
                        [part],
                        anywhere=range(3, len(inputs)),
                        name="double_states",
                    )
                ahead.append(swap(total, (2 * step - 1) * low * group, devices))
                step *= 2
        else:
            ahead = climb(level + 1, low * group, folded)
        inputs = [rates] + states + ahead + (beside["spread"] if level == 1 else [])
        outs = call(
            functools.partial(spread_kernel, sizes, level, span, forward),
            inputs,
            [jax.ShapeDtypeStruct((heads,) + state, BF16)] * group,
            anywhere=range(1 + group + len(ahead), len(inputs)),
            name="spread_states",
        )
        return [outs[0]] + [swap(outs[k], k * low, devices) for k in range(1, group)]

    return climb(1, sizes[0], parts)


def local(devices, queries, key_vectors, value_vectors, output_grad, decay_rate, norm_gain):
    length, heads, size = queries.shape
    half = heads // 2
    sizes = level_sizes(devices)
    parts = sizes[1]

    def shaped(*shape, dtype=BF16):
        return jax.ShapeDtypeStruct(shape, dtype)

    per_head = shaped(half, length, size)
    per_head_wide = shaped(half, length, size, dtype=F32)
    states = shaped(half, size, size)
    part_states = shaped(half // parts, size, size)
    whole = shaped(length, heads, size)
    block = shaped(length, half, size)
    flat_rows = shaped(length * half, size, dtype=F32)
    flat = pltpu.VMEM((length * half, size), F32)
    stage = pltpu.VMEM((length, half, size), BF16)
    copy_sem = pltpu.SemaphoreType.DMA
    sems = copy_sem((2, CHUNKS))
    unit = 2 * half * length * size * size
    span = float(length)

    sent_key, sent_value, sent_state, key_rest, value_rest, rates = call(
        first_local_kernel,
        [key_vectors, value_vectors, decay_rate],
        [per_head, per_head, states, block, block, shaped(heads, size, dtype=F32)],
        [stage, stage, flat, flat, pltpu.SMEM((heads,), F32), sems, copy_sem((2,)), copy_sem],
        outside=(0, 1, 2),
        limit=LOCAL_LIMIT,
        flops=unit,
        name="local_states",
    )
    kept_key, kept_value, kept_state = call(
        second_local_kernel,
        [key_rest, value_rest, rates],
        [per_head, per_head, states],
        [flat, flat],
        flops=unit,
        name="local_states",
    )
    keys, values = [kept_key, sent_key], [kept_value, sent_value]
    other_state = swap(sent_state, 1, devices)
    query, normal, attention, inner = [None, None], [None, None], [None, None], [None, None]
    gains = norm_gain
    for s in (0, 1):
        query[s], *normal[s], attention[s], inner[s], gains = call(
            functools.partial(attention_kernel, s == 0),
            [queries, output_grad, keys[s], values[s], rates, gains],
            [per_head, per_head, shaped(half, size, length), per_head_wide]
            + [shaped(half, length, length), per_head_wide, shaped(heads, size, dtype=F32)],
            [flat, flat],
            flops=2 * unit,
            name="attention",
        )
    folded = {}
    for ks in ((parts - 1,), range(parts - 1)):
        inputs = [rates, kept_state, other_state] + list(folded.values())
        parts_here = call(
            functools.partial(pair_fold_kernel, sizes, ks, span, True),
            inputs,
            [part_states] * len(ks),
            anywhere=range(3, len(inputs)),
            name="fold_pair",
        )
        folded.update(zip(ks, parts_here))
    before = carry_states(
        folded, sizes, devices, rates, length, True, {"fold": inner[:1], "double": [], "spread": inner[1:]}
    )

    stages = [(0, parts - 1), range(1, parts - 1)]

    def spread_pair(ks, forward, before, kept, other, beside):
        inputs = [rates, kept, other] + [before[k] for k in ks] + beside
        stage_states = shaped(half // parts * len(ks), size, size)
        return call(
            functools.partial(pair_spread_kernel, sizes, ks, span, forward),
            inputs,
            [stage_states] * 2,
            anywhere=range(3 + len(ks), len(inputs)),
            name="spread_pair",
        )

    made, folded, kept_grads, other_grads = [[], []], {}, [], []
    for ks in stages:
        send, mine = spread_pair(ks, True, before, kept_state, other_state, made[0][:1])
        grads = []
        for s, incoming in ((0, mine), (1, swap(send, 1, devices))):
            inputs = [*normal[s], inner[s], incoming, gains]
            *made[s], state_grad = call(
                functools.partial(norm_kernel, s == 0, sizes, ks),
                inputs + made[s],
                [per_head, per_head, states, send],
                aliases={len(inputs) + n: n for n in range(len(made[s]))},
                flops=unit,
                name="norm",
            )
            grads.append(state_grad)
        kept_grads.append(grads[1])
        other_grads.append(swap(grads[0], 1, devices))
        inputs = [rates, kept_grads[-1], other_grads[-1]] + list(folded.values())[-1:]
        parts_here = call(
            functools.partial(pair_fold_kernel, sizes, ks, span, False),
            inputs,
            [part_states] * len(ks),
            anywhere=range(3, len(inputs)),
            name="fold_pair",
        )
        folded.update(zip(ks, parts_here))
    normed_out, query_out = None, None
    key_part, value_part, key_decayed, value_decayed, marks = [None] * 2, [None] * 2, [None] * 2, [None] * 2, []
    for s in (0, 1):
        normed, grad_out, incoming = made[s]
        scores, key_part[s], value_part[s], key_decayed[s], value_decayed[s] = call(
            functools.partial(inner_kernel, s == 0),
            [query[s], keys[s], values[s], attention[s], grad_out, rates],
            [shaped(half, length, length), per_head_wide, per_head_wide, per_head, per_head],
            flops=3 * unit,
            name="inner_gradients",
        )
        inputs = [keys[s], scores, grad_out, incoming, normed, rates]
        count = len(inputs)
        aliases = {}
        if s:
            aliases = {count: 0, count + 1: 1}
            inputs += [normed_out, query_out]
        normed_out, query_out, mark = call(
            functools.partial(query_kernel, s == 0),
            inputs,
            [whole, whole, shaped(8, size, dtype=F32)],
            [flat, flat, stage, stage, sems],
            outside=(count, count + 1),
            out_outside=(0, 1),
            aliases=aliases,
            flops=2 * unit,
            name="query_gradient",
        )
        marks.append(mark)
    after = carry_states(
        folded,
        sizes,
        devices,
        rates,
        length,
        False,
        {"fold": key_part, "double": marks[:1], "spread": marks[1:]},
    )
    flats = [[], []]
    for n, ks in enumerate(stages):
        send, mine = spread_pair(ks, False, after, kept_grads[n], other_grads[n], flats[1][:1])
        for s, later in ((1, mine), (0, swap(send, 1, devices))):
            inputs = [key_decayed[s], value_decayed[s], later, key_part[s], value_part[s]]
            if s == 0 and n:
                break
            flats[s] = call(
                functools.partial(later_kernel, sizes, ks),
                inputs + flats[s],
                [flat_rows, flat_rows],
                aliases={len(inputs) + m: m for m in range(len(flats[s]))},
                flops=unit,
                name="later_gradients",
            )
    inputs += call(join_kernel, flats[1], [block, block], name="join_heads")
    key_out, value_out, *_ = call(
        functools.partial(last_kernel, True, sizes, stages[-1]),
        inputs + flats[0],
        [whole, whole, flat_rows, flat_rows],
        [stage, stage, copy_sem((3, CHUNKS))],
        out_outside=(0, 1),
        aliases={len(inputs) + n: 2 + n for n in range(2)},
        flops=unit,
        name="last_gradients",
    )
    return normed_out, query_out, key_out, value_out


def solution(mesh):
    devices = mesh.shape["ctx"] * mesh.shape["head"]
    spread = P(AXES, None, None)
    return jax.shard_map(
        functools.partial(local, devices),
        mesh=mesh,
        in_specs=(spread, spread, spread, spread, P(), P()),
        out_specs=(spread, spread, spread, spread),
        check_vma=False,
    )
```

```python
import functools
import jax
import jax.numpy as jnp
from jax import lax
from jax.experimental import pallas as pl
from jax.experimental.pallas import tpu as pltpu
from jax.sharding import PartitionSpec as P

AXES = ("ctx", "head")
F32 = jnp.float32
BF16 = jnp.bfloat16
VMEM_LIMIT = 16 * 1024 * 1024
LOCAL_LIMIT = 51 * 1024 * 1024
BATCH = 16
CHUNKS = 4


def dot(a, b, dims):
    return lax.dot_general(a, b, (dims, ((), ())), preferred_element_type=F32)


AB = ((1,), (0,))
ABT = ((1,), (1,))
ATB = ((0,), (0,))


def decay(rate, steps):
    return jnp.exp(-rate * steps)


def positions(shape):
    return lax.broadcasted_iota(jnp.int32, shape, 0).astype(F32)


def causal_weights(rate, length):
    row = lax.broadcasted_iota(jnp.int32, (length, length), 0)
    col = lax.broadcasted_iota(jnp.int32, (length, length), 1)
    offset = (row - col).astype(F32)
    return jnp.where(offset >= 0, jnp.exp(-rate * jnp.maximum(offset, 0.0)), 0.0)


def my_index():
    return lax.axis_index("ctx") * lax.axis_size("head") + lax.axis_index("head")


def head_half(own):
    core = my_index() % 2
    return core if own else 1 - core


def split_heads(block_ref, scratch, half, heads):
    length, _, size = block_ref.shape
    start = pl.multiple_of(half * heads, heads)
    scratch[...] = block_ref[:, pl.ds(start, heads), :].astype(F32).reshape(length * heads, size)


def one_head(scratch, h, length, heads):
    return scratch[pl.ds(h, length, stride=heads), :]


def start_output(scratch, stage, out_ref, sems, half):
    length, heads, size = stage.shape
    chunks = sems.shape[0]
    rows = length // chunks
    start = pl.multiple_of(half * heads, heads)
    copies = []
    for c in range(chunks):
        piece = pl.ds(c * rows, rows)
        stage[piece] = scratch[pl.ds(c * rows * heads, rows * heads), :].reshape(rows, heads, size).astype(BF16)
        copy = pltpu.make_async_copy(stage.at[piece], out_ref.at[piece, pl.ds(start, heads), :], sems.at[c])
        copy.start()
        copies.append(copy)
    return copies


def batches(heads, size=BATCH):
    size = min(size, heads)
    return [range(start, start + size) for start in range(0, heads, size)]


def local_states(key, value, rate_ref, first, s_ref):
    heads, length, size = key.shape
    tail_steps = length - 1.0 - positions((length, size))
    for batch in batches(heads):
        tail = [decay(rate_ref[pl.ds(first + h, 1), :], tail_steps) for h in batch]
        decayed = [(key[h].astype(F32) * t).astype(BF16) for h, t in zip(batch, tail)]
        state = [dot(k, value[h], ATB) for h, k in zip(batch, decayed)]
        for i, h in enumerate(batch):
            s_ref[h] = state[i].astype(BF16)


def to_heads(flat, out_ref):
    heads, length, _ = out_ref.shape
    for h in range(heads):
        out_ref[h] = one_head(flat, h, length, heads).astype(BF16)


def bring_kernel(k_ref, v_ref, kt_ref, vt_ref, k_rest, v_rest, *scratch):
    kb, vb, ks, vs, sems, rest_sems = scratch
    length, heads, size = kb.shape
    half = head_half(False)
    start = pl.multiple_of(half * heads, heads)
    rest = pl.multiple_of((1 - half) * heads, heads)
    chunks = sems.shape[1]
    rows = length // chunks
    copies = []
    for c in range(chunks):
        piece = pl.ds(c * rows, rows)
        for n, (ref, buffer) in enumerate(((k_ref, kb), (v_ref, vb))):
            copy = pltpu.make_async_copy(ref.at[piece, pl.ds(start, heads), :], buffer.at[piece], sems.at[n, c])
            copy.start()
            copies.append(copy)
    rest_copies = []
    for n, (ref, buffer) in enumerate(((k_ref, k_rest), (v_ref, v_rest))):
        copy = pltpu.make_async_copy(ref.at[:, pl.ds(rest, heads), :], buffer, rest_sems.at[n])
        copy.start()
        rest_copies.append(copy)
    for c in range(chunks):
        piece = pl.ds(c * rows, rows)
        flat = pl.ds(c * rows * heads, rows * heads)
        copies[2 * c].wait()
        ks[flat, :] = kb[piece].astype(F32).reshape(rows * heads, size)
        copies[2 * c + 1].wait()
        vs[flat, :] = vb[piece].astype(F32).reshape(rows * heads, size)
    to_heads(ks, kt_ref)
    to_heads(vs, vt_ref)
    for copy in rest_copies:
        copy.wait()


def first_local_kernel(kt_ref, vt_ref, rate_ref, s_ref):
    local_states(kt_ref, vt_ref, rate_ref, head_half(False) * kt_ref.shape[0], s_ref)


def second_local_kernel(k_ref, v_ref, rate_ref, kt_ref, vt_ref, s_ref, ks, vs):
    heads, length, size = kt_ref.shape
    ks[...] = k_ref[...].astype(F32).reshape(length * heads, size)
    vs[...] = v_ref[...].astype(F32).reshape(length * heads, size)
    to_heads(ks, kt_ref)
    to_heads(vs, vt_ref)
    local_states(kt_ref, vt_ref, rate_ref, head_half(True) * heads, s_ref)


def attention_kernel(own, q_ref, g_ref, kt_ref, vt_ref, rate_ref, gain_ref, *rest):
    qt_ref, qd_ref, qd_across_ref, scaled_ref, a_ref, o_ref, gain_out, qs, gs = rest
    gain_out[...] = gain_ref[...]
    heads, length, size = kt_ref.shape
    half = head_half(own)
    first = half * heads
    split_heads(q_ref, qs, half, heads)
    split_heads(g_ref, gs, half, heads)
    head_steps = positions((length, size)) + 1.0
    for batch in batches(heads):
        rate = [rate_ref[pl.ds(first + h, 1), :] for h in batch]
        wide = [one_head(qs, h, length, heads) for h in batch]
        query = [q.astype(BF16) for q in wide]
        decayed = [(q * decay(r, head_steps)).astype(BF16) for q, r in zip(wide, rate)]
        scores = [dot(q, kt_ref[h], ABT) for q, h in zip(query, batch)]
        weights = [causal_weights(r, length) for r in rate]
        attention = [(s * w).astype(BF16) for s, w in zip(scores, weights)]
        inner = [dot(a, vt_ref[h], AB) for a, h in zip(attention, batch)]
        for i, h in enumerate(batch):
            qt_ref[h] = query[i]
            qd_ref[h] = decayed[i]
            qd_across_ref[h] = decayed[i].T
            scaled_ref[h] = gain_ref[pl.ds(first + h, 1), :] * one_head(gs, h, length, heads)
            a_ref[h] = attention[i]
            o_ref[h] = inner[i]


def norm_kernel(own, sizes, ks, qd_ref, qd_across_ref, scaled_ref, o_ref, in_ref, gain_ref, *rest):
    n_ref, go_ref, all_in_ref, sg_ref = rest[-4:]
    first = head_half(own) * qd_ref.shape[0]
    places = part_heads_of(sizes, ks, in_ref.shape[0])
    for batch in batches(len(places)):
        out = [o_ref[places[h]] + dot(qd_ref[places[h]], in_ref[h], AB) for h in batch]
        inv_rms = [lax.rsqrt(jnp.mean(o * o, axis=-1, keepdims=True) + 1e-06) for o in out]
        unit = [o * r for o, r in zip(out, inv_rms)]
        gain = [gain_ref[pl.ds(first + places[h], 1), :] for h in batch]
        scaled = [scaled_ref[places[h]] for h in batch]
        along = [jnp.mean(s * u, axis=-1, keepdims=True) for s, u in zip(scaled, unit)]
        grad_out = [
            (r * (s - u * m)).astype(BF16) for r, s, u, m in zip(inv_rms, scaled, unit, along)
        ]
        state = [dot(qd_across_ref[places[h]], g, AB) for h, g in zip(batch, grad_out)]
        for i, h in enumerate(batch):
            n_ref[places[h]] = (unit[i] * gain[i]).astype(BF16)
            go_ref[places[h]] = grad_out[i]
            all_in_ref[places[h]] = in_ref[h]
            sg_ref[h] = state[i].astype(BF16)


def inner_kernel(own, qt_ref, kt_ref, vt_ref, a_ref, go_ref, rate_ref, gs_ref, dk_ref, dv_ref, kd_ref, vd_ref):
    heads, length, size = qt_ref.shape
    tail_steps = length - 1.0 - positions((length, size))
    first = head_half(own) * heads
    for batch in batches(heads):
        inner = [dot(go_ref[h], vt_ref[h], ABT) for h in batch]
        value = [dot(a_ref[h], go_ref[h], ATB) for h in batch]
        weights = [causal_weights(rate_ref[pl.ds(first + h, 1), :], length) for h in batch]
        scores = [(s * w).astype(BF16) for s, w in zip(inner, weights)]
        key = [dot(s, qt_ref[h], ATB) for s, h in zip(scores, batch)]
        for i, h in enumerate(batch):
            gs_ref[h] = scores[i]
            dv_ref[h] = value[i]
            dk_ref[h] = key[i]
            tail = decay(rate_ref[pl.ds(first + h, 1), :], tail_steps)
            kd_ref[h] = (kt_ref[h].astype(F32) * tail).astype(BF16)
            vd_ref[h] = (vt_ref[h].astype(F32) * tail).astype(BF16)


def query_kernel(own, kt_ref, gs_ref, go_ref, in_ref, n_ref, rate_ref, *rest):
    n_out, dq_out, mark_ref, ns, ds, nb, db, sems = rest[-8:]
    mark_ref[...] = jnp.zeros(mark_ref.shape, F32)
    heads, length, size = kt_ref.shape
    half = head_half(own)
    first = half * heads
    head_steps = positions((length, size)) + 1.0
    for h in range(heads):
        ns[pl.ds(h, length, stride=heads), :] = n_ref[h].astype(F32)
    copies = start_output(ns, nb, n_out, sems.at[0], half)
    for batch in batches(heads):
        through = [dot(go_ref[h], in_ref[h], ABT) for h in batch]
        query = [dot(gs_ref[h], kt_ref[h], AB) for h in batch]
        for i, h in enumerate(batch):
            head_decay = decay(rate_ref[pl.ds(first + h, 1), :], head_steps)
            ds[pl.ds(h, length, stride=heads), :] = query[i] + head_decay * through[i]
    copies += start_output(ds, db, dq_out, sems.at[1], half)
    for copy in copies:
        copy.wait()


def add_later(sizes, ks, kd_ref, vd_ref, later_ref, dk_ref, dv_ref, keys, values):
    heads, length, size = kd_ref.shape
    places = part_heads_of(sizes, ks, later_ref.shape[0])
    for batch in batches(len(places)):
        key = [dot(vd_ref[places[h]], later_ref[h], ABT) for h in batch]
        value = [dot(kd_ref[places[h]], later_ref[h], AB) for h in batch]
        for i, h in enumerate(batch):
            at = places[h]
            keys[pl.ds(at, length, stride=heads), :] = dk_ref[at] + key[i]
            values[pl.ds(at, length, stride=heads), :] = dv_ref[at] + value[i]


def later_kernel(sizes, ks, *refs):
    add_later(sizes, ks, *refs[:5], *refs[-2:])


def join_kernel(ks, vs, k_ref, v_ref):
    rows = pl.ds(0, k_ref.shape[0] * k_ref.shape[1])
    k_ref[...] = ks[rows, :].reshape(k_ref.shape).astype(BF16)
    v_ref[...] = vs[rows, :].reshape(v_ref.shape).astype(BF16)


def last_kernel(own, sizes, parts, *refs):
    k_rest, v_rest = refs[5:7]
    dk_out, dv_out, ks, vs, kb, vb, sems = refs[-7:]
    heads = kb.shape[1]
    half = head_half(own)
    start = pl.multiple_of((1 - half) * heads, heads)
    copies = []
    for n, (block, out) in enumerate(((k_rest, dk_out), (v_rest, dv_out))):
        copy = pltpu.make_async_copy(block, out.at[:, pl.ds(start, heads), :], sems.at[2, n])
        copy.start()
        copies.append(copy)
    add_later(sizes, parts, *refs[:5], ks, vs)
    copies += start_output(ks, kb, dk_out, sems.at[0], half)
    copies += start_output(vs, vb, dv_out, sems.at[1], half)
    for copy in copies:
        copy.wait()


def row_weight(rate, span, steps):
    weight = jnp.exp(-rate * (span * jnp.maximum(steps, 0).astype(F32)))
    return jnp.where(steps >= 0, weight, 0.0)


def place_at(sizes, level, forward=True):
    low = 1
    for size in sizes[:level]:
        low *= size
    place = (my_index() // low) % sizes[level]
    return place if forward else place ^ (sizes[level] - 1)


def first_head(sizes, level, heads, forward):
    first, count = 0, heads
    for above in range(level + 1):
        count //= sizes[above]
        place = place_at(sizes, above)
        if above == 0 and not forward:
            place = 1 - place
        first = first + place * count
    return first


def part_start(sizes, k, heads):
    return (place_at(sizes, 1) ^ k) * heads


def part_heads_of(sizes, ks, count):
    part = count // len(ks)
    return [part_start(sizes, k, part) + i for k in ks for i in range(part)]


def fold_kernel(sizes, level, span, forward, rate_ref, *refs):
    group = sizes[level]
    top = level + 2 == len(sizes)
    count = 1 if top else sizes[level + 1]
    states, parts = refs[:group], refs[len(refs) - count :]
    heads = parts[0].shape[0]
    first = first_head(sizes, level, rate_ref.shape[0], forward)
    place = place_at(sizes, level, forward)
    weigh = [group - 1 - (place ^ j) for j in range(group)]
    for k in range(count):
        start = 0 if top else (place_at(sizes, level + 1) ^ k) * heads
        for i in range(heads):
            rate = rate_ref[pl.ds(first + start + i, 1), :]
            total = None
            for j in range(group):
                term = row_weight(rate, span, weigh[j]) * states[j][start + i].astype(F32)
                total = term if total is None else total + term
            parts[k][i] = total.astype(BF16)


def pair_fold_kernel(sizes, ks, span, forward, rate_ref, kept_ref, other_ref, *rest):
    out_refs = rest[len(rest) - len(ks) :]
    first = first_head(sizes, 0, rate_ref.shape[0], forward)
    place = place_at(sizes, 0, forward)
    part = out_refs[0].shape[0]
    for i, head in enumerate(part_heads_of(sizes, ks, part * len(ks))):
        at = head if kept_ref.shape[0] > part * len(ks) else i
        rate = rate_ref[pl.ds(first + head, 1), :]
        total = row_weight(rate, span, 1 - place) * kept_ref[at].astype(F32)
        total = total + row_weight(rate, span, place) * other_ref[at].astype(F32)
        out_refs[i // part][i % part] = total.astype(BF16)


def double_kernel(sizes, level, step, span, forward, rate_ref, state_ref, other_ref, *rest):
    out_ref = rest[-1]
    first = first_head(sizes, level - 1, rate_ref.shape[0], forward)
    upper = (place_at(sizes, level, forward) // step) % 2
    for i in range(out_ref.shape[0]):
        rate = rate_ref[pl.ds(first + i, 1), :]
        total = row_weight(rate, span * step, 1 - upper) * state_ref[i].astype(F32)
        total = total + row_weight(rate, span * step, upper) * other_ref[i].astype(F32)
        out_ref[i] = total.astype(BF16)


def spread_kernel(sizes, level, span, forward, rate_ref, *refs):
    group, next_group = sizes[level], sizes[level + 1]
    top = level + 2 == len(sizes)
    count = 1 if top else next_group
    ahead_count = next_group.bit_length() - 1 if top else next_group
    states, ahead, outs = refs[:group], refs[group : group + ahead_count], refs[len(refs) - group :]
    heads = states[0].shape[0]
    part_heads = heads // count
    first = first_head(sizes, level, rate_ref.shape[0], forward)
    place = place_at(sizes, level, forward)
    top_place = place_at(sizes, level + 1, forward)
    for k in range(count):
        start = 0 if top else (place_at(sizes, level + 1) ^ k) * part_heads
        for i in range(part_heads):
            rate = rate_ref[pl.ds(first + start + i, 1), :]
            if top:
                before = None
                for j in range(ahead_count):
                    step = 1 << j
                    steps = jnp.where((top_place // step) % 2 == 1, top_place % step, -1)
                    term = row_weight(rate, span * group, steps) * ahead[j][i].astype(F32)
                    before = term if before is None else before + term
            else:
                before = ahead[k][i].astype(F32)
            own = [states[j][start + i].astype(F32) for j in range(group)]
            for j in range(group):
                total = row_weight(rate, span, place ^ j) * before
                for q in range(group):
                    if q != j:
                        total = total + row_weight(rate, span, (place ^ j) - 1 - (place ^ q)) * own[q]
                outs[j][start + i] = total.astype(BF16)


def pair_spread_kernel(sizes, ks, span, forward, rate_ref, kept_ref, other_ref, *rest):
    before_refs, (send_ref, mine_ref) = rest[: len(ks)], rest[-2:]
    count = send_ref.shape[0]
    part = count // len(ks)
    first = first_head(sizes, 0, rate_ref.shape[0], forward)
    place = place_at(sizes, 0, forward)
    for i, head in enumerate(part_heads_of(sizes, ks, count)):
        at = head if kept_ref.shape[0] > count else i
        rate = rate_ref[pl.ds(first + head, 1), :]
        before = before_refs[i // part][i % part].astype(F32)
        onward = row_weight(rate, span, 1) * before
        send = onward + kept_ref[at].astype(F32)
        send_ref[i] = jnp.where(place == 0, send, before).astype(BF16)
        mine = onward + other_ref[at].astype(F32)
        mine_ref[i] = jnp.where(place == 0, before, mine).astype(BF16)


WHOLE = pl.BlockSpec(memory_space=pltpu.VMEM)
ANYWHERE = pl.BlockSpec(memory_space=pl.ANY)
OUTSIDE = pl.BlockSpec(memory_space=pltpu.HBM)


def call(body, inputs, outputs, scratch=(), anywhere=(), outside=(), out_outside=(), aliases=None, flops=0, name=None, limit=VMEM_LIMIT, count_bytes=True):
    nbytes = sum(a.size * a.dtype.itemsize for a in inputs) + sum(s.size * s.dtype.itemsize for s in outputs)
    nbytes = nbytes if count_bytes else 0
    return list(pl.pallas_call(
        body,
        in_specs=[ANYWHERE if n in anywhere else OUTSIDE if n in outside else WHOLE for n in range(len(inputs))],
        out_specs=[OUTSIDE if n in out_outside else WHOLE for n in range(len(outputs))],
        scratch_shapes=list(scratch),
        out_shape=list(outputs),
        input_output_aliases=aliases or {},
        compiler_params=pltpu.CompilerParams(vmem_limit_bytes=limit),
        cost_estimate=pl.CostEstimate(flops=flops, bytes_accessed=nbytes, transcendentals=0),
        name=name,
    )(*inputs))


def level_sizes(devices):
    sizes = [2]
    left = devices // 2
    while left > 8:
        sizes.append(4)
        left //= 4
    return sizes + [left]


def swap(array, distance, devices):
    return lax.ppermute(array, AXES, [(i, i ^ distance) for i in range(devices)])


def carry_states(parts, sizes, devices, rates, length, forward, beside):
    state = parts[0].shape[1:]

    def climb(level, low, parts):
        group, next_group = sizes[level], sizes[level + 1]
        top = level + 2 == len(sizes)
        span = float(length * low)
        states = [parts[0]] + [swap(parts[k], k * low, devices) for k in range(1, group)]
        heads = parts[0].shape[0]
        count = 1 if top else next_group
        part = jax.ShapeDtypeStruct((heads // count,) + state, BF16)
        inputs = [rates] + states + (beside["fold"] if level == 1 else [])
        folded = call(
            functools.partial(fold_kernel, sizes, level, span, forward),
            inputs,
            [part] * count,
            anywhere=range(1 + group, len(inputs)),
            name="fold_states",
        )
        if top:
            total, ahead, step = folded[0], [], 1
            while step < next_group:
                if step > 1:
                    inputs = [rates, total, ahead[-1]] + (beside["double"] if step == 2 else [])
                    (total,) = call(
                        functools.partial(
                            double_kernel, sizes, level + 1, step // 2, span * group, forward
                        ),
                        inputs,
                        [part],
                        anywhere=range(3, len(inputs)),
                        name="double_states",
                    )
                ahead.append(swap(total, (2 * step - 1) * low * group, devices))
                step *= 2
        else:
            ahead = climb(level + 1, low * group, folded)
        inputs = [rates] + states + ahead + (beside["spread"] if level == 1 else [])
        outs = call(
            functools.partial(spread_kernel, sizes, level, span, forward),
            inputs,
            [jax.ShapeDtypeStruct((heads,) + state, BF16)] * group,
            anywhere=range(1 + group + len(ahead), len(inputs)),
            name="spread_states",
        )
        return [outs[0]] + [swap(outs[k], k * low, devices) for k in range(1, group)]

    return climb(1, sizes[0], parts)


def local(devices, queries, key_vectors, value_vectors, output_grad, decay_rate, norm_gain):
    length, heads, size = queries.shape
    half = heads // 2
    sizes = level_sizes(devices)
    parts = sizes[1]

    def shaped(*shape, dtype=BF16):
        return jax.ShapeDtypeStruct(shape, dtype)

    per_head = shaped(half, length, size)
    per_head_wide = shaped(half, length, size, dtype=F32)
    states = shaped(half, size, size)
    part_states = shaped(half // parts, size, size)
    whole = shaped(length, heads, size)
    block = shaped(length, half, size)
    flat_rows = shaped((length + 1) * half, size, dtype=F32)
    flat = pltpu.VMEM((length * half, size), F32)
    stage = pltpu.VMEM((length, half, size), BF16)
    copy_sem = pltpu.SemaphoreType.DMA
    sems = copy_sem((2, CHUNKS))
    unit = 2 * half * length * size * size
    span = float(length)

    rates = jnp.broadcast_to(decay_rate[:, None], (heads, size))
    sent_key, sent_value, key_rest, value_rest = call(
        bring_kernel,
        [key_vectors, value_vectors],
        [per_head, per_head, block, block],
        [stage, stage, flat, flat, copy_sem((2, 2)), copy_sem((2,))],
        outside=(0, 1),
        limit=LOCAL_LIMIT,
        name="keys_and_values",
    )
    (sent_state,) = call(
        first_local_kernel,
        [sent_key, sent_value, rates],
        [states],
        flops=unit,
        name="local_states",
    )
    kept_key, kept_value, kept_state = call(
        second_local_kernel,
        [key_rest, value_rest, rates],
        [per_head, per_head, states],
        [flat, flat],
        flops=unit,
        name="local_states",
    )
    keys, values = [kept_key, sent_key], [kept_value, sent_value]
    other_state = swap(sent_state, 1, devices)
    query, normal, attention, inner = [None, None], [None, None], [None, None], [None, None]
    gains = norm_gain
    for s in (0, 1):
        query[s], *normal[s], attention[s], inner[s], gains = call(
            functools.partial(attention_kernel, s == 0),
            [queries, output_grad, keys[s], values[s], rates, gains],
            [per_head, per_head, shaped(half, size, length), per_head_wide]
            + [shaped(half, length, length), per_head_wide, shaped(heads, size, dtype=F32)],
            [flat, flat],
            flops=2 * unit,
            name="attention",
        )
    folded = {}
    for ks in ((2, 3), (0, 1)):
        inputs = [rates, kept_state, other_state] + list(folded.values())
        parts_here = call(
            functools.partial(pair_fold_kernel, sizes, ks, span, True),
            inputs,
            [part_states] * len(ks),
            anywhere=range(3, len(inputs)),
            name="fold_pair",
        )
        folded.update(zip(ks, parts_here))
    before = carry_states(
        folded, sizes, devices, rates, length, True, {"fold": inner[:1], "double": [], "spread": inner[1:]}
    )

    stages = [(0, parts - 1), range(1, parts - 1)]

    def spread_pair(ks, forward, before, kept, other, beside):
        inputs = [rates, kept, other] + [before[k] for k in ks] + beside
        stage_states = shaped(half // parts * len(ks), size, size)
        return call(
            functools.partial(pair_spread_kernel, sizes, ks, span, forward),
            inputs,
            [stage_states] * 2,
            anywhere=range(3 + len(ks), len(inputs)),
            name="spread_pair",
        )

    made, folded, kept_grads, other_grads = [[], []], {}, [], []
    for ks in stages:
        send, mine = spread_pair(ks, True, before, kept_state, other_state, made[0][:1])
        grads = []
        for s, incoming in ((0, mine), (1, swap(send, 1, devices))):
            inputs = [*normal[s], inner[s], incoming, gains]
            *made[s], state_grad = call(
                functools.partial(norm_kernel, s == 0, sizes, ks),
                inputs + made[s],
                [per_head, per_head, states, send],
                aliases={len(inputs) + n: n for n in range(len(made[s]))},
                flops=unit,
                name="norm",
            )
            grads.append(state_grad)
        kept_grads.append(grads[1])
        other_grads.append(swap(grads[0], 1, devices))
        inputs = [rates, kept_grads[-1], other_grads[-1]] + list(folded.values())[-1:]
        parts_here = call(
            functools.partial(pair_fold_kernel, sizes, ks, span, False),
            inputs,
            [part_states] * len(ks),
            anywhere=range(3, len(inputs)),
            name="fold_pair",
        )
        folded.update(zip(ks, parts_here))
    normed_out, query_out = None, None
    key_part, value_part, key_decayed, value_decayed, marks = [None] * 2, [None] * 2, [None] * 2, [None] * 2, []
    for s in (0, 1):
        normed, grad_out, incoming = made[s]
        scores, key_part[s], value_part[s], key_decayed[s], value_decayed[s] = call(
            functools.partial(inner_kernel, s == 0),
            [query[s], keys[s], values[s], attention[s], grad_out, rates],
            [shaped(half, length, length), per_head_wide, per_head_wide, per_head, per_head],
            flops=3 * unit,
            name="inner_gradients",
        )
        inputs = [keys[s], scores, grad_out, incoming, normed, rates]
        count = len(inputs)
        aliases = {}
        if s:
            aliases = {count: 0, count + 1: 1}
            inputs += [normed_out, query_out]
        normed_out, query_out, mark = call(
            functools.partial(query_kernel, s == 0),
            inputs,
            [whole, whole, shaped(8, size, dtype=F32)],
            [flat, flat, stage, stage, sems],
            outside=(count, count + 1),
            out_outside=(0, 1),
            aliases=aliases,
            flops=2 * unit,
            name="query_gradient",
        )
        marks.append(mark)
    after = carry_states(
        folded,
        sizes,
        devices,
        rates,
        length,
        False,
        {"fold": key_part, "double": marks[:1], "spread": marks[1:]},
    )
    flats = [[], []]
    for n, ks in enumerate(stages):
        send, mine = spread_pair(ks, False, after, kept_grads[n], other_grads[n], flats[1][:1])
        for s, later in ((1, mine), (0, swap(send, 1, devices))):
            inputs = [key_decayed[s], value_decayed[s], later, key_part[s], value_part[s]]
            if s == 0 and n:
                break
            flats[s] = call(
                functools.partial(later_kernel, sizes, ks),
                inputs + flats[s],
                [flat_rows, flat_rows],
                aliases={len(inputs) + m: m for m in range(len(flats[s]))},
                flops=unit,
                name="later_gradients",
            )
    inputs += call(join_kernel, flats[1], [block, block], name="join_heads")
    key_out, value_out, *_ = call(
        functools.partial(last_kernel, True, sizes, stages[-1]),
        inputs + flats[0],
        [whole, whole, flat_rows, flat_rows],
        [stage, stage, copy_sem((3, CHUNKS))],
        out_outside=(0, 1),
        aliases={len(inputs) + n: 2 + n for n in range(2)},
        flops=unit,
        name="last_gradients",
    )
    return normed_out, query_out, key_out, value_out


def solution(mesh):
    devices = mesh.shape["ctx"] * mesh.shape["head"]
    spread = P(AXES, None, None)
    return jax.shard_map(
        functools.partial(local, devices),
        mesh=mesh,
        in_specs=(spread, spread, spread, spread, P(), P()),
        out_specs=(spread, spread, spread, spread),
        check_vma=False,
    )
```

```python
import functools
import jax
import jax.numpy as jnp
from jax import lax
from jax.experimental import pallas as pl
from jax.experimental.pallas import tpu as pltpu
from jax.sharding import PartitionSpec as P

AXES = ("ctx", "head")
F32 = jnp.float32
BF16 = jnp.bfloat16
VMEM_LIMIT = 16 * 1024 * 1024
LOCAL_LIMIT = 51 * 1024 * 1024
BATCH = 16
CHUNKS = 4


def dot(a, b, dims):
    return lax.dot_general(a, b, (dims, ((), ())), preferred_element_type=F32)


AB = ((1,), (0,))
ABT = ((1,), (1,))
ATB = ((0,), (0,))


def decay(rate, steps):
    return jnp.exp(-rate * steps)


def positions(shape):
    return lax.broadcasted_iota(jnp.int32, shape, 0).astype(F32)


def causal_weights(rate, length):
    row = lax.broadcasted_iota(jnp.int32, (length, length), 0)
    col = lax.broadcasted_iota(jnp.int32, (length, length), 1)
    offset = (row - col).astype(F32)
    return jnp.where(offset >= 0, jnp.exp(-rate * jnp.maximum(offset, 0.0)), 0.0)


def my_index():
    return lax.axis_index("ctx") * lax.axis_size("head") + lax.axis_index("head")


def head_half(own):
    core = my_index() % 2
    return core if own else 1 - core


def split_heads(block_ref, scratch, half, heads):
    length, _, size = block_ref.shape
    start = pl.multiple_of(half * heads, heads)
    scratch[...] = block_ref[:, pl.ds(start, heads), :].astype(F32).reshape(length * heads, size)


def one_head(scratch, h, length, heads):
    return scratch[pl.ds(h, length, stride=heads), :]


def start_output(scratch, stage, out_ref, sems, half):
    length, heads, size = stage.shape
    chunks = sems.shape[0]
    rows = length // chunks
    start = pl.multiple_of(half * heads, heads)
    copies = []
    for c in range(chunks):
        piece = pl.ds(c * rows, rows)
        stage[piece] = scratch[pl.ds(c * rows * heads, rows * heads), :].reshape(rows, heads, size).astype(BF16)
        copy = pltpu.make_async_copy(stage.at[piece], out_ref.at[piece, pl.ds(start, heads), :], sems.at[c])
        copy.start()
        copies.append(copy)
    return copies


def batches(heads, size=BATCH):
    size = min(size, heads)
    return [range(start, start + size) for start in range(0, heads, size)]


def local_states(key, value, rate_ref, first, s_ref):
    heads, length, size = key.shape
    tail_steps = length - 1.0 - positions((length, size))
    for batch in batches(heads):
        tail = [decay(rate_ref[pl.ds(first + h, 1), :], tail_steps) for h in batch]
        decayed = [(key[h].astype(F32) * t).astype(BF16) for h, t in zip(batch, tail)]
        state = [dot(k, value[h], ATB) for h, k in zip(batch, decayed)]
        for i, h in enumerate(batch):
            s_ref[h] = state[i].astype(BF16)


def to_heads(flat, out_ref):
    heads, length, _ = out_ref.shape
    for h in range(heads):
        out_ref[h] = one_head(flat, h, length, heads).astype(BF16)


def bring_kernel(k_ref, v_ref, kt_ref, vt_ref, k_rest, v_rest, *scratch):
    kb, vb, ks, vs, sems, rest_sems = scratch
    length, heads, size = kb.shape
    half = head_half(False)
    start = pl.multiple_of(half * heads, heads)
    rest = pl.multiple_of((1 - half) * heads, heads)
    chunks = sems.shape[1]
    rows = length // chunks
    copies = []
    for n, (ref, buffer) in enumerate(((k_ref, kb), (v_ref, vb))):
        for c in range(chunks):
            piece = pl.ds(c * rows, rows)
            copy = pltpu.make_async_copy(ref.at[piece, pl.ds(start, heads), :], buffer.at[piece], sems.at[n, c])
            copy.start()
            copies.append(copy)
    rest_copies = []
    for n, (ref, buffer) in enumerate(((k_ref, k_rest), (v_ref, v_rest))):
        copy = pltpu.make_async_copy(ref.at[:, pl.ds(rest, heads), :], buffer, rest_sems.at[n])
        copy.start()
        rest_copies.append(copy)
    for n, (buffer, flat, out) in enumerate(((kb, ks, kt_ref), (vb, vs, vt_ref))):
        for c in range(chunks):
            copies[n * chunks + c].wait()
            piece = pl.ds(c * rows, rows)
            flat[pl.ds(c * rows * heads, rows * heads), :] = buffer[piece].astype(F32).reshape(rows * heads, size)
        to_heads(flat, out)
    for copy in rest_copies:
        copy.wait()


def first_local_kernel(kt_ref, vt_ref, rate_ref, s_ref):
    local_states(kt_ref, vt_ref, rate_ref, head_half(False) * kt_ref.shape[0], s_ref)


def second_local_kernel(k_ref, v_ref, rate_ref, kt_ref, vt_ref, s_ref, ks, vs):
    heads, length, size = kt_ref.shape
    ks[...] = k_ref[...].astype(F32).reshape(length * heads, size)
    vs[...] = v_ref[...].astype(F32).reshape(length * heads, size)
    to_heads(ks, kt_ref)
    to_heads(vs, vt_ref)
    local_states(kt_ref, vt_ref, rate_ref, head_half(True) * heads, s_ref)


def attention_kernel(own, q_ref, g_ref, kt_ref, vt_ref, rate_ref, gain_ref, *rest):
    qt_ref, qd_ref, qd_across_ref, scaled_ref, a_ref, o_ref, gain_out, qs, gs = rest
    gain_out[...] = gain_ref[...]
    heads, length, size = kt_ref.shape
    half = head_half(own)
    first = half * heads
    split_heads(q_ref, qs, half, heads)
    split_heads(g_ref, gs, half, heads)
    head_steps = positions((length, size)) + 1.0
    for batch in batches(heads):
        rate = [rate_ref[pl.ds(first + h, 1), :] for h in batch]
        wide = [one_head(qs, h, length, heads) for h in batch]
        query = [q.astype(BF16) for q in wide]
        decayed = [(q * decay(r, head_steps)).astype(BF16) for q, r in zip(wide, rate)]
        scores = [dot(q, kt_ref[h], ABT) for q, h in zip(query, batch)]
        weights = [causal_weights(r, length) for r in rate]
        attention = [(s * w).astype(BF16) for s, w in zip(scores, weights)]
        inner = [dot(a, vt_ref[h], AB) for a, h in zip(attention, batch)]
        for i, h in enumerate(batch):
            qt_ref[h] = query[i]
            qd_ref[h] = decayed[i]
            qd_across_ref[h] = decayed[i].T
            scaled_ref[h] = gain_ref[pl.ds(first + h, 1), :] * one_head(gs, h, length, heads)
            a_ref[h] = attention[i]
            o_ref[h] = inner[i]


def norm_kernel(own, sizes, ks, qd_ref, qd_across_ref, scaled_ref, o_ref, in_ref, gain_ref, *rest):
    n_ref, go_ref, all_in_ref, sg_ref = rest[-4:]
    first = head_half(own) * qd_ref.shape[0]
    places = part_heads_of(sizes, ks, in_ref.shape[0])
    for batch in batches(len(places)):
        out = [o_ref[places[h]] + dot(qd_ref[places[h]], in_ref[h], AB) for h in batch]
        inv_rms = [lax.rsqrt(jnp.mean(o * o, axis=-1, keepdims=True) + 1e-06) for o in out]
        unit = [o * r for o, r in zip(out, inv_rms)]
        gain = [gain_ref[pl.ds(first + places[h], 1), :] for h in batch]
        scaled = [scaled_ref[places[h]] for h in batch]
        along = [jnp.mean(s * u, axis=-1, keepdims=True) for s, u in zip(scaled, unit)]
        grad_out = [
            (r * (s - u * m)).astype(BF16) for r, s, u, m in zip(inv_rms, scaled, unit, along)
        ]
        state = [dot(qd_across_ref[places[h]], g, AB) for h, g in zip(batch, grad_out)]
        for i, h in enumerate(batch):
            n_ref[places[h]] = (unit[i] * gain[i]).astype(BF16)
            go_ref[places[h]] = grad_out[i]
            all_in_ref[places[h]] = in_ref[h]
            sg_ref[h] = state[i].astype(BF16)


def inner_kernel(own, qt_ref, kt_ref, vt_ref, a_ref, go_ref, rate_ref, gs_ref, dk_ref, dv_ref, kd_ref, vd_ref):
    heads, length, size = qt_ref.shape
    tail_steps = length - 1.0 - positions((length, size))
    first = head_half(own) * heads
    for batch in batches(heads):
        inner = [dot(go_ref[h], vt_ref[h], ABT) for h in batch]
        value = [dot(a_ref[h], go_ref[h], ATB) for h in batch]
        weights = [causal_weights(rate_ref[pl.ds(first + h, 1), :], length) for h in batch]
        scores = [(s * w).astype(BF16) for s, w in zip(inner, weights)]
        key = [dot(s, qt_ref[h], ATB) for s, h in zip(scores, batch)]
        for i, h in enumerate(batch):
            gs_ref[h] = scores[i]
            dv_ref[h] = value[i]
            dk_ref[h] = key[i]
            tail = decay(rate_ref[pl.ds(first + h, 1), :], tail_steps)
            kd_ref[h] = (kt_ref[h].astype(F32) * tail).astype(BF16)
            vd_ref[h] = (vt_ref[h].astype(F32) * tail).astype(BF16)


def query_kernel(own, kt_ref, gs_ref, go_ref, in_ref, n_ref, rate_ref, *rest):
    n_out, dq_out, mark_ref, ns, ds, nb, db, sems = rest[-8:]
    mark_ref[...] = jnp.zeros(mark_ref.shape, F32)
    heads, length, size = kt_ref.shape
    half = head_half(own)
    first = half * heads
    head_steps = positions((length, size)) + 1.0
    for h in range(heads):
        ns[pl.ds(h, length, stride=heads), :] = n_ref[h].astype(F32)
    copies = start_output(ns, nb, n_out, sems.at[0], half)
    for batch in batches(heads):
        through = [dot(go_ref[h], in_ref[h], ABT) for h in batch]
        query = [dot(gs_ref[h], kt_ref[h], AB) for h in batch]
        for i, h in enumerate(batch):
            head_decay = decay(rate_ref[pl.ds(first + h, 1), :], head_steps)
            ds[pl.ds(h, length, stride=heads), :] = query[i] + head_decay * through[i]
    copies += start_output(ds, db, dq_out, sems.at[1], half)
    for copy in copies:
        copy.wait()


def add_later(sizes, ks, kd_ref, vd_ref, later_ref, dk_ref, dv_ref, keys, values):
    heads, length, size = kd_ref.shape
    places = part_heads_of(sizes, ks, later_ref.shape[0])
    for batch in batches(len(places)):
        key = [dot(vd_ref[places[h]], later_ref[h], ABT) for h in batch]
        value = [dot(kd_ref[places[h]], later_ref[h], AB) for h in batch]
        for i, h in enumerate(batch):
            at = places[h]
            keys[pl.ds(at, length, stride=heads), :] = dk_ref[at] + key[i]
            values[pl.ds(at, length, stride=heads), :] = dv_ref[at] + value[i]


def later_kernel(sizes, ks, *refs):
    add_later(sizes, ks, *refs[:5], *refs[-2:])


def join_kernel(ks, vs, k_ref, v_ref):
    rows = pl.ds(0, k_ref.shape[0] * k_ref.shape[1])
    k_ref[...] = ks[rows, :].reshape(k_ref.shape).astype(BF16)
    v_ref[...] = vs[rows, :].reshape(v_ref.shape).astype(BF16)


def last_kernel(own, sizes, parts, *refs):
    k_rest, v_rest = refs[5:7]
    dk_out, dv_out, ks, vs, kb, vb, sems = refs[-7:]
    heads = kb.shape[1]
    half = head_half(own)
    start = pl.multiple_of((1 - half) * heads, heads)
    copies = []
    for n, (block, out) in enumerate(((k_rest, dk_out), (v_rest, dv_out))):
        copy = pltpu.make_async_copy(block, out.at[:, pl.ds(start, heads), :], sems.at[2, n])
        copy.start()
        copies.append(copy)
    add_later(sizes, parts, *refs[:5], ks, vs)
    copies += start_output(ks, kb, dk_out, sems.at[0], half)
    copies += start_output(vs, vb, dv_out, sems.at[1], half)
    for copy in copies:
        copy.wait()


def row_weight(rate, span, steps):
    weight = jnp.exp(-rate * (span * jnp.maximum(steps, 0).astype(F32)))
    return jnp.where(steps >= 0, weight, 0.0)


def place_at(sizes, level, forward=True):
    low = 1
    for size in sizes[:level]:
        low *= size
    place = (my_index() // low) % sizes[level]
    return place if forward else place ^ (sizes[level] - 1)


def first_head(sizes, level, heads, forward):
    first, count = 0, heads
    for above in range(level + 1):
        count //= sizes[above]
        place = place_at(sizes, above)
        if above == 0 and not forward:
            place = 1 - place
        first = first + place * count
    return first


def part_start(sizes, k, heads):
    return (place_at(sizes, 1) ^ k) * heads


def part_heads_of(sizes, ks, count):
    part = count // len(ks)
    return [part_start(sizes, k, part) + i for k in ks for i in range(part)]


def fold_kernel(sizes, level, span, forward, rate_ref, *refs):
    group = sizes[level]
    top = level + 2 == len(sizes)
    count = 1 if top else sizes[level + 1]
    states, parts = refs[:group], refs[len(refs) - count :]
    heads = parts[0].shape[0]
    first = first_head(sizes, level, rate_ref.shape[0], forward)
    place = place_at(sizes, level, forward)
    weigh = [group - 1 - (place ^ j) for j in range(group)]
    for k in range(count):
        start = 0 if top else (place_at(sizes, level + 1) ^ k) * heads
        for i in range(heads):
            rate = rate_ref[pl.ds(first + start + i, 1), :]
            total = None
            for j in range(group):
                term = row_weight(rate, span, weigh[j]) * states[j][start + i].astype(F32)
                total = term if total is None else total + term
            parts[k][i] = total.astype(BF16)


def pair_fold_kernel(sizes, ks, span, forward, rate_ref, kept_ref, other_ref, *rest):
    out_refs = rest[len(rest) - len(ks) :]
    first = first_head(sizes, 0, rate_ref.shape[0], forward)
    place = place_at(sizes, 0, forward)
    part = out_refs[0].shape[0]
    for i, head in enumerate(part_heads_of(sizes, ks, part * len(ks))):
        at = head if kept_ref.shape[0] > part * len(ks) else i
        rate = rate_ref[pl.ds(first + head, 1), :]
        total = row_weight(rate, span, 1 - place) * kept_ref[at].astype(F32)
        total = total + row_weight(rate, span, place) * other_ref[at].astype(F32)
        out_refs[i // part][i % part] = total.astype(BF16)


def double_kernel(sizes, level, step, span, forward, rate_ref, state_ref, other_ref, *rest):
    out_ref = rest[-1]
    first = first_head(sizes, level - 1, rate_ref.shape[0], forward)
    upper = (place_at(sizes, level, forward) // step) % 2
    for i in range(out_ref.shape[0]):
        rate = rate_ref[pl.ds(first + i, 1), :]
        total = row_weight(rate, span * step, 1 - upper) * state_ref[i].astype(F32)
        total = total + row_weight(rate, span * step, upper) * other_ref[i].astype(F32)
        out_ref[i] = total.astype(BF16)


def spread_kernel(sizes, level, span, forward, rate_ref, *refs):
    group, next_group = sizes[level], sizes[level + 1]
    top = level + 2 == len(sizes)
    count = 1 if top else next_group
    ahead_count = next_group.bit_length() - 1 if top else next_group
    states, ahead, outs = refs[:group], refs[group : group + ahead_count], refs[len(refs) - group :]
    heads = states[0].shape[0]
    part_heads = heads // count
    first = first_head(sizes, level, rate_ref.shape[0], forward)
    place = place_at(sizes, level, forward)
    top_place = place_at(sizes, level + 1, forward)
    for k in range(count):
        start = 0 if top else (place_at(sizes, level + 1) ^ k) * part_heads
        for i in range(part_heads):
            rate = rate_ref[pl.ds(first + start + i, 1), :]
            if top:
                before = None
                for j in range(ahead_count):
                    step = 1 << j
                    steps = jnp.where((top_place // step) % 2 == 1, top_place % step, -1)
                    term = row_weight(rate, span * group, steps) * ahead[j][i].astype(F32)
                    before = term if before is None else before + term
            else:
                before = ahead[k][i].astype(F32)
            own = [states[j][start + i].astype(F32) for j in range(group)]
            for j in range(group):
                total = row_weight(rate, span, place ^ j) * before
                for q in range(group):
                    if q != j:
                        total = total + row_weight(rate, span, (place ^ j) - 1 - (place ^ q)) * own[q]
                outs[j][start + i] = total.astype(BF16)


def pair_spread_kernel(sizes, ks, span, forward, rate_ref, kept_ref, other_ref, *rest):
    before_refs, (send_ref, mine_ref) = rest[: len(ks)], rest[-2:]
    count = send_ref.shape[0]
    part = count // len(ks)
    first = first_head(sizes, 0, rate_ref.shape[0], forward)
    place = place_at(sizes, 0, forward)
    for i, head in enumerate(part_heads_of(sizes, ks, count)):
        at = head if kept_ref.shape[0] > count else i
        rate = rate_ref[pl.ds(first + head, 1), :]
        before = before_refs[i // part][i % part].astype(F32)
        onward = row_weight(rate, span, 1) * before
        send = onward + kept_ref[at].astype(F32)
        send_ref[i] = jnp.where(place == 0, send, before).astype(BF16)
        mine = onward + other_ref[at].astype(F32)
        mine_ref[i] = jnp.where(place == 0, before, mine).astype(BF16)


WHOLE = pl.BlockSpec(memory_space=pltpu.VMEM)
ANYWHERE = pl.BlockSpec(memory_space=pl.ANY)
OUTSIDE = pl.BlockSpec(memory_space=pltpu.HBM)


def call(body, inputs, outputs, scratch=(), anywhere=(), outside=(), out_outside=(), aliases=None, flops=0, name=None, limit=VMEM_LIMIT, count_bytes=True):
    nbytes = sum(a.size * a.dtype.itemsize for a in inputs) + sum(s.size * s.dtype.itemsize for s in outputs)
    nbytes = nbytes if count_bytes else 0
    return list(pl.pallas_call(
        body,
        in_specs=[ANYWHERE if n in anywhere else OUTSIDE if n in outside else WHOLE for n in range(len(inputs))],
        out_specs=[OUTSIDE if n in out_outside else WHOLE for n in range(len(outputs))],
        scratch_shapes=list(scratch),
        out_shape=list(outputs),
        input_output_aliases=aliases or {},
        compiler_params=pltpu.CompilerParams(vmem_limit_bytes=limit),
        cost_estimate=pl.CostEstimate(flops=flops, bytes_accessed=nbytes, transcendentals=0),
        name=name,
    )(*inputs))


def level_sizes(devices):
    sizes = [2]
    left = devices // 2
    while left > 8:
        sizes.append(4)
        left //= 4
    return sizes + [left]


def swap(array, distance, devices):
    return lax.ppermute(array, AXES, [(i, i ^ distance) for i in range(devices)])


def carry_states(parts, sizes, devices, rates, length, forward, beside):
    state = parts[0].shape[1:]

    def climb(level, low, parts):
        group, next_group = sizes[level], sizes[level + 1]
        top = level + 2 == len(sizes)
        span = float(length * low)
        states = [parts[0]] + [swap(parts[k], k * low, devices) for k in range(1, group)]
        heads = parts[0].shape[0]
        count = 1 if top else next_group
        part = jax.ShapeDtypeStruct((heads // count,) + state, BF16)
        inputs = [rates] + states + (beside["fold"] if level == 1 else [])
        folded = call(
            functools.partial(fold_kernel, sizes, level, span, forward),
            inputs,
            [part] * count,
            anywhere=range(1 + group, len(inputs)),
            name="fold_states",
        )
        if top:
            total, ahead, step = folded[0], [], 1
            while step < next_group:
                if step > 1:
                    inputs = [rates, total, ahead[-1]] + (beside["double"] if step == 2 else [])
                    (total,) = call(
                        functools.partial(
                            double_kernel, sizes, level + 1, step // 2, span * group, forward
                        ),
                        inputs,
                        [part],
                        anywhere=range(3, len(inputs)),
                        name="double_states",
                    )
                ahead.append(swap(total, (2 * step - 1) * low * group, devices))
                step *= 2
        else:
            ahead = climb(level + 1, low * group, folded)
        inputs = [rates] + states + ahead + (beside["spread"] if level == 1 else [])
        outs = call(
            functools.partial(spread_kernel, sizes, level, span, forward),
            inputs,
            [jax.ShapeDtypeStruct((heads,) + state, BF16)] * group,
            anywhere=range(1 + group + len(ahead), len(inputs)),
            name="spread_states",
        )
        return [outs[0]] + [swap(outs[k], k * low, devices) for k in range(1, group)]

    return climb(1, sizes[0], parts)


def local(devices, queries, key_vectors, value_vectors, output_grad, decay_rate, norm_gain):
    length, heads, size = queries.shape
    half = heads // 2
    sizes = level_sizes(devices)
    parts = sizes[1]

    def shaped(*shape, dtype=BF16):
        return jax.ShapeDtypeStruct(shape, dtype)

    per_head = shaped(half, length, size)
    per_head_wide = shaped(half, length, size, dtype=F32)
    states = shaped(half, size, size)
    part_states = shaped(half // parts, size, size)
    whole = shaped(length, heads, size)
    block = shaped(length, half, size)
    flat_rows = shaped((length + 1) * half, size, dtype=F32)
    flat = pltpu.VMEM((length * half, size), F32)
    stage = pltpu.VMEM((length, half, size), BF16)
    copy_sem = pltpu.SemaphoreType.DMA
    sems = copy_sem((2, CHUNKS))
    unit = 2 * half * length * size * size
    span = float(length)

    rates = jnp.broadcast_to(decay_rate[:, None], (heads, size))
    sent_key, sent_value, key_rest, value_rest = call(
        bring_kernel,
        [key_vectors, value_vectors],
        [per_head, per_head, block, block],
        [stage, stage, flat, flat, copy_sem((2, 2)), copy_sem((2,))],
        outside=(0, 1),
        limit=LOCAL_LIMIT,
        name="keys_and_values",
    )
    (sent_state,) = call(
        first_local_kernel,
        [sent_key, sent_value, rates],
        [states],
        flops=unit,
        name="local_states",
    )
    kept_key, kept_value, kept_state = call(
        second_local_kernel,
        [key_rest, value_rest, rates],
        [per_head, per_head, states],
        [flat, flat],
        flops=unit,
        name="local_states",
    )
    keys, values = [kept_key, sent_key], [kept_value, sent_value]
    other_state = swap(sent_state, 1, devices)
    query, normal, attention, inner = [None, None], [None, None], [None, None], [None, None]
    gains = norm_gain
    for s in (0, 1):
        query[s], *normal[s], attention[s], inner[s], gains = call(
            functools.partial(attention_kernel, s == 0),
            [queries, output_grad, keys[s], values[s], rates, gains],
            [per_head, per_head, shaped(half, size, length), per_head_wide]
            + [shaped(half, length, length), per_head_wide, shaped(heads, size, dtype=F32)],
            [flat, flat],
            flops=2 * unit,
            name="attention",
        )
    folded = {}
    for ks in ((2, 3), (0, 1)):
        inputs = [rates, kept_state, other_state] + list(folded.values())
        parts_here = call(
            functools.partial(pair_fold_kernel, sizes, ks, span, True),
            inputs,
            [part_states] * len(ks),
            anywhere=range(3, len(inputs)),
            name="fold_pair",
        )
        folded.update(zip(ks, parts_here))
    before = carry_states(
        folded, sizes, devices, rates, length, True, {"fold": inner[:1], "double": [], "spread": inner[1:]}
    )

    stages = [(0, parts - 1), range(1, parts - 1)]

    def spread_pair(ks, forward, before, kept, other, beside):
        inputs = [rates, kept, other] + [before[k] for k in ks] + beside
        stage_states = shaped(half // parts * len(ks), size, size)
        return call(
            functools.partial(pair_spread_kernel, sizes, ks, span, forward),
            inputs,
            [stage_states] * 2,
            anywhere=range(3 + len(ks), len(inputs)),
            name="spread_pair",
        )

    made, folded, kept_grads, other_grads = [[], []], {}, [], []
    for ks in stages:
        send, mine = spread_pair(ks, True, before, kept_state, other_state, made[0][:1])
        grads = []
        for s, incoming in ((0, mine), (1, swap(send, 1, devices))):
            inputs = [*normal[s], inner[s], incoming, gains]
            *made[s], state_grad = call(
                functools.partial(norm_kernel, s == 0, sizes, ks),
                inputs + made[s],
                [per_head, per_head, states, send],
                aliases={len(inputs) + n: n for n in range(len(made[s]))},
                flops=unit,
                name="norm",
            )
            grads.append(state_grad)
        kept_grads.append(grads[1])
        other_grads.append(swap(grads[0], 1, devices))
        inputs = [rates, kept_grads[-1], other_grads[-1]] + list(folded.values())[-1:]
        parts_here = call(
            functools.partial(pair_fold_kernel, sizes, ks, span, False),
            inputs,
            [part_states] * len(ks),
            anywhere=range(3, len(inputs)),
            name="fold_pair",
        )
        folded.update(zip(ks, parts_here))
    normed_out, query_out = None, None
    key_part, value_part, key_decayed, value_decayed, marks = [None] * 2, [None] * 2, [None] * 2, [None] * 2, []
    for s in (0, 1):
        normed, grad_out, incoming = made[s]
        scores, key_part[s], value_part[s], key_decayed[s], value_decayed[s] = call(
            functools.partial(inner_kernel, s == 0),
            [query[s], keys[s], values[s], attention[s], grad_out, rates],
            [shaped(half, length, length), per_head_wide, per_head_wide, per_head, per_head],
            flops=3 * unit,
            name="inner_gradients",
        )
        inputs = [keys[s], scores, grad_out, incoming, normed, rates]
        count = len(inputs)
        aliases = {}
        if s:
            aliases = {count: 0, count + 1: 1}
            inputs += [normed_out, query_out]
        normed_out, query_out, mark = call(
            functools.partial(query_kernel, s == 0),
            inputs,
            [whole, whole, shaped(8, size, dtype=F32)],
            [flat, flat, stage, stage, sems],
            outside=(count, count + 1),
            out_outside=(0, 1),
            aliases=aliases,
            flops=2 * unit,
            name="query_gradient",
        )
        marks.append(mark)
    after = carry_states(
        folded,
        sizes,
        devices,
        rates,
        length,
        False,
        {"fold": key_part, "double": marks[:1], "spread": marks[1:]},
    )
    flats = [[], []]
    for n, ks in enumerate(stages):
        send, mine = spread_pair(ks, False, after, kept_grads[n], other_grads[n], flats[1][:1])
        for s, later in ((1, mine), (0, swap(send, 1, devices))):
            inputs = [key_decayed[s], value_decayed[s], later, key_part[s], value_part[s]]
            if s == 0 and n:
                break
            flats[s] = call(
                functools.partial(later_kernel, sizes, ks),
                inputs + flats[s],
                [flat_rows, flat_rows],
                aliases={len(inputs) + m: m for m in range(len(flats[s]))},
                flops=unit,
                name="later_gradients",
            )
    inputs += call(join_kernel, flats[1], [block, block], name="join_heads")
    key_out, value_out, *_ = call(
        functools.partial(last_kernel, True, sizes, stages[-1]),
        inputs + flats[0],
        [whole, whole, flat_rows, flat_rows],
        [stage, stage, copy_sem((3, CHUNKS))],
        out_outside=(0, 1),
        aliases={len(inputs) + n: 2 + n for n in range(2)},
        flops=unit,
        name="last_gradients",
    )
    return normed_out, query_out, key_out, value_out


def solution(mesh):
    devices = mesh.shape["ctx"] * mesh.shape["head"]
    spread = P(AXES, None, None)
    return jax.shard_map(
        functools.partial(local, devices),
        mesh=mesh,
        in_specs=(spread, spread, spread, spread, P(), P()),
        out_specs=(spread, spread, spread, spread),
        check_vma=False,
    )
```
